32 devices in a mesh: flt: 8 (over y, x, core), scn: 4 (over z).
Axes of the slice: x: 2, y: 2, z: 4, core: 2. Of those that a mesh axis runs over, the one named last changes fastest.
Arguments:
- tiles: bfloat16 [384, 128, 128], P('flt'), as said below
- tile_row: int32 [384], P('flt'), may hold values from 0 to 7, as said below
- tile_col: int32 [384], P('flt'), may hold values from 0 to 7, as said below
- tile_count: int32 [8], P('flt'), may hold values from 16 to 48, as said below
- slot_offset: int32 [8192], P('flt'), may hold values from 0 to 19
- capacity: int32 [128, 1024], P('scn', 'flt'), may hold values from 0 to 999
- plan0: float32 [8192], P('flt'), may hold values from 0 to 1
- hold0: float32 [128, 8192], P('scn', 'flt'), may hold values from 0 to 2
- dual0: float32 [128, 1024], P('scn', 'flt'), may hold values from 0 to 1
Outputs:
- plan: float32 [8192], P('flt')
- hold: float32 [128, 8192], P('scn', 'flt')
- dual: float32 [128, 1024], P('scn', 'flt')
The draws below stay inside these ranges and needn't reach their ends.
Inputs may be any that keep to these rules, and one draw needn't show every extreme that they name: `tile_col`: the live slots of every flt index name each of its 8 column blocks. `tile_row`: the live slots of all flt indices together name every row block. `tile_count`: some flt index has exactly 16 live slots and some other has all 48. `tiles`: entries are finite; slots from `tile_count` on may hold any finite values and are ignored.
All inputs are finite; a program needn't handle non-finite values.
Results may differ from the reference program's by a relative error of at most 0.00155.
The reference program's roundings to bfloat16 on the way (of `matrix` and `mixed`) count: a program that leaves them out, or rounds other values in their place, can miss the bound.
Values may be sent and summed in bfloat16 or wider, within the bound.
No kernel may reach another device: no remote copies, remote signals or barrier semaphores. Data moves between devices by JAX's collectives and lax.ppermute only.
A program may use at most 64 MiB of HBM per device.

```python
import math
import jax
import jax.numpy as jnp
from jax import lax

BLOCK = 128
OPTIONS = 20
CB_DEV = 8
TILE_CAP = 48
SWEEPS = 4
ITERS = 2
RB = 8
ROWS = 1024
NCOL = 8192
SCEN = 128
TILE_ALL = 384


def tile_layout(key):
    index = jnp.arange(TILE_ALL, dtype=jnp.int32)
    slot = index % TILE_CAP
    owner = index // TILE_CAP
    rows = jax.random.randint(jax.random.fold_in(key, 11), (TILE_ALL,), 0, RB)
    cols = jax.random.randint(jax.random.fold_in(key, 12), (TILE_ALL,), 0, CB_DEV)
    base = slot < CB_DEV
    rows = jnp.where(base, (owner * CB_DEV + slot) % RB, rows)
    cols = jnp.where(base, slot, cols)
    return (rows.astype(jnp.int32), cols.astype(jnp.int32))


def draw_tile_row(key, part):
    return tile_layout(key)[0]


def draw_tile_col(key, part):
    return tile_layout(key)[1]


def draw_tile_count(key, part):
    groups = TILE_ALL // TILE_CAP
    counts = jax.random.randint(jax.random.fold_in(key, 21), (groups,), TILE_CAP // 3, TILE_CAP + 1)
    busiest = jax.random.randint(jax.random.fold_in(key, 22), (), 0, groups)
    lightest = (busiest + 1) % groups
    position = jnp.arange(groups)
    counts = jnp.where(position == lightest, TILE_CAP // 3, counts)
    return jnp.where(position == busiest, TILE_CAP, counts).astype(jnp.int32)


def draw_tiles(key, part):
    first = jax.random.fold_in(key, 31)
    second = jax.random.fold_in(key, 32)
    third = jax.random.fold_in(key, 33)
    fourth = jax.random.fold_in(key, 34)
    fifth = jax.random.fold_in(key, 35)
    base = jax.random.normal(first, (TILE_ALL, BLOCK, BLOCK), jnp.float32)
    top = 10.0
    row_spread = jnp.exp(jax.random.uniform(second, (TILE_ALL, BLOCK, 1), jnp.float32, 0.0, math.log(top)))
    col_spread = jnp.exp(jax.random.uniform(third, (TILE_ALL, 1, BLOCK), jnp.float32, 0.0, math.log(top)))
    rows, cols = tile_layout(key)
    index = jnp.arange(TILE_ALL, dtype=jnp.int32)
    owner = index // TILE_CAP
    global_col = (owner * CB_DEV + cols).astype(jnp.int32)
    col_blocks = TILE_ALL // TILE_CAP * CB_DEV
    reach = math.log(40.0)
    row_level = jnp.exp(jax.random.uniform(fourth, (RB,), jnp.float32, -reach, reach))
    col_level = jnp.exp(jax.random.uniform(fifth, (col_blocks,), jnp.float32, -reach, reach))
    factor = jnp.take(row_level, rows, axis=0) * jnp.take(col_level, global_col, axis=0)
    return (base * row_spread * col_spread * factor[:, None, None]).astype(jnp.bfloat16)


def draw_slot_offset(key, part):
    index = jnp.arange(NCOL, dtype=jnp.int32)
    upper = 5 + 15 * index // NCOL
    values = jax.random.randint(key, (NCOL,), 0, upper)
    values = values.at[0].set(0).at[NCOL - 1].set(OPTIONS - 1)
    return values.astype(jnp.int32)


def draw_capacity(key, part):
    index = jnp.arange(ROWS, dtype=jnp.int32)
    upper = 300 + 700 * index // ROWS
    values = jax.random.randint(key, (SCEN, ROWS), 0, upper[None, :])
    values = values.at[0, 0].set(0).at[SCEN - 1, ROWS - 1].set(999)
    return values.astype(jnp.int32)


def block_levels(key, extent, shards, smallest, high):
    gain, own = 1.0, jax.random.fold_in(key, 6)
    for axis_at, shards_of in shards:
        draws = jnp.exp(jax.random.uniform(jax.random.fold_in(own, axis_at), (shards_of,), jnp.float32, smallest / len(shards), high / len(shards)))
        gain = gain * jnp.repeat(draws, extent[axis_at] // shards_of).reshape([-1 if axis == axis_at else 1 for axis in range(len(extent))])
    return gain


def setup_inputs(seed: int = 0) -> dict:
    splits = jax.random.split(jax.random.key(seed), 10)
    return {
        "tiles": draw_tiles(jax.random.fold_in(splits[9], 71), 0),
        "tile_row": draw_tile_row(jax.random.fold_in(splits[9], 71), 0),
        "tile_col": draw_tile_col(jax.random.fold_in(splits[9], 71), 0),
        "tile_count": draw_tile_count(jax.random.fold_in(splits[9], 71), 0),
        "slot_offset": draw_slot_offset(jax.random.fold_in(splits[9], 71), 0),
        "capacity": draw_capacity(jax.random.fold_in(splits[9], 71), 0),
        "plan0": jnp.clip(1.0 * jax.random.uniform(splits[6], (NCOL,), jnp.float32) ** block_levels(splits[6], (NCOL,), ((0, 8),), -0.2, 0.2), 0.0, 1.0),
        "hold0": jnp.clip(2.0 * jax.random.uniform(splits[7], (SCEN, NCOL), jnp.float32) ** block_levels(splits[7], (SCEN, NCOL), ((0, 4), (1, 8)), -0.2, 0.2), 0.0, 2.0),
        "dual0": jnp.clip(1.0 * jax.random.uniform(splits[8], (SCEN, ROWS), jnp.float32) ** block_levels(splits[8], (SCEN, ROWS), ((0, 4), (1, 8)), -0.2, 0.2), 0.0, 1.0),
    }


EPS = 1e-06
COST_RATE = 1.0
HOLD_BASE = 1.0
HOLD_CAP = 2.0
CAP_UNIT = 4.0
TAU_PLAN = 0.2
TAU_HOLD = 0.02
SIGMA = 0.05

def pull_columns(matrix, tile_row, tile_col, dual_low):
    blocks = dual_low.astype(jnp.float32).reshape(SCEN, RB, BLOCK)
    groups = matrix.reshape(-1, TILE_CAP, BLOCK, BLOCK)
    rows = tile_row.reshape(-1, TILE_CAP)
    cols = tile_col.reshape(-1, TILE_CAP)

    def one_group(parts):
        tiles_here, rows_here, cols_here = parts
        picked = jnp.take(blocks, rows_here, axis=1)
        product = jnp.einsum('stk,tkj->tsj', picked, tiles_here.astype(jnp.float32))
        total = jax.ops.segment_sum(product, cols_here, num_segments=CB_DEV)
        return jnp.transpose(total, (1, 0, 2)).reshape(SCEN, CB_DEV * BLOCK)
    result = lax.map(one_group, (groups, rows, cols))
    return jnp.transpose(result, (1, 0, 2)).reshape(SCEN, -1)

def push_rows(matrix, tile_row, tile_col, mixed_low):
    blocks = mixed_low.astype(jnp.float32).reshape(SCEN, -1, BLOCK)
    groups = matrix.reshape(-1, TILE_CAP, BLOCK, BLOCK)
    rows = tile_row.reshape(-1, TILE_CAP)
    cols = tile_col.reshape(-1, TILE_CAP)
    owners = jnp.arange(groups.shape[0], dtype=jnp.int32)

    def one_group(carry, parts):
        tiles_here, rows_here, cols_here, owner = parts
        picked = jnp.take(blocks, (owner * CB_DEV + cols_here).astype(jnp.int32), axis=1)
        product = jnp.einsum('tkj,stj->tsk', tiles_here.astype(jnp.float32), picked)
        return (carry + jax.ops.segment_sum(product, rows_here, num_segments=RB), None)
    start = jnp.zeros((RB, SCEN, BLOCK), jnp.float32)
    total, _ = lax.scan(one_group, start, (groups, rows, cols, owners))
    return jnp.transpose(total, (1, 0, 2)).reshape(SCEN, ROWS)

def reference(tiles, tile_row, tile_col, tile_count, slot_offset, capacity, plan0, hold0, dual0):
    index = jnp.arange(TILE_ALL, dtype=jnp.int32)
    owner = index // TILE_CAP
    live = (index % TILE_CAP < tile_count[owner]).astype(jnp.float32)
    global_col = (owner * CB_DEV + tile_col).astype(jnp.int32)
    col_blocks = NCOL // BLOCK
    magnitude = jnp.abs(tiles.astype(jnp.float32)) * live[:, None, None]
    scale_row = jnp.ones((RB, BLOCK), jnp.float32)
    scale_col = jnp.ones((col_blocks, BLOCK), jnp.float32)
    for sweep in range(SWEEPS):
        row_factor = jnp.take(scale_row, tile_row, axis=0)
        col_factor = jnp.take(scale_col, global_col, axis=0)
        scaled = magnitude * row_factor[:, :, None] * col_factor[:, None, :]
        row_peak = jax.ops.segment_max(lax.optimization_barrier(jnp.max(scaled, axis=2)), tile_row, num_segments=RB)
        col_peak = jax.ops.segment_max(lax.optimization_barrier(jnp.max(scaled, axis=1)), global_col, num_segments=col_blocks)
        scale_row = scale_row / jnp.sqrt(row_peak + EPS)
        scale_col = scale_col / jnp.sqrt(col_peak + EPS)
    row_factor = jnp.take(scale_row, tile_row, axis=0)
    col_factor = jnp.take(scale_col, global_col, axis=0)
    matrix = (tiles.astype(jnp.float32) * live[:, None, None] * row_factor[:, :, None] * col_factor[:, None, :]).astype(jnp.bfloat16)
    col_scale = scale_col.reshape(-1)
    row_scale = scale_row.reshape(-1)
    offsets = slot_offset.astype(jnp.float32)
    cost = COST_RATE * offsets * col_scale
    hold_cost = (HOLD_BASE + COST_RATE * offsets) * col_scale
    demand = CAP_UNIT * capacity.astype(jnp.float32) * row_scale[None, :]
    plan = plan0 / col_scale
    hold = hold0 / col_scale[None, :]
    dual = dual0 / row_scale[None, :]
    plan_top = 1.0 / col_scale
    hold_top = HOLD_CAP / col_scale
    for step in range(ITERS):
        grad = pull_columns(matrix, tile_row, tile_col, dual.astype(jnp.bfloat16))
        mean_grad = lax.optimization_barrier(jnp.sum(grad, axis=0)) / SCEN
        plan_next = jnp.clip(plan - TAU_PLAN * (cost + mean_grad), 0.0, plan_top)
        hold_next = jnp.clip(hold - TAU_HOLD * (hold_cost[None, :] + grad), 0.0, hold_top[None, :])
        mixed = ((2.0 * plan_next - plan)[None, :] + (2.0 * hold_next - hold)).astype(jnp.bfloat16)
        load = push_rows(matrix, tile_row, tile_col, mixed)
        dual = jnp.maximum(dual + SIGMA * (load - demand), 0.0)
        plan, hold = (plan_next, hold_next)
    return (plan * col_scale, hold * col_scale[None, :], dual * row_scale[None, :])
```

```python
import functools

import jax
import jax.numpy as jnp
from jax import lax
from jax.experimental import pallas as pl
from jax.experimental.pallas import tpu as pltpu
from jax.sharding import PartitionSpec as P

EPS = 1e-06
COST_RATE = 1.0
HOLD_BASE = 1.0
HOLD_CAP = 2.0
CAP_UNIT = 4.0
TAU_PLAN = 0.2
TAU_HOLD = 0.02
SIGMA = 0.05

B = 128
UNROLL = 4
VMEM = pl.BlockSpec(memory_space=pltpu.VMEM)
SMEM = pl.BlockSpec(memory_space=pltpu.SMEM)
F32 = jnp.float32
BF16 = jnp.bfloat16


def call(body, out_shape, scratch, n_smem, n_vmem):
    return pl.pallas_call(
        body,
        out_shape=out_shape,
        in_specs=[SMEM] * n_smem + [VMEM] * n_vmem,
        out_specs=[VMEM] * len(out_shape),
        scratch_shapes=scratch,
        compiler_params=pltpu.CompilerParams(vmem_limit_bytes=24 * 1024 * 1024),
    )


def loop(count, step):
    def trip(i, carry):
        for u in range(UNROLL):
            step(i * UNROLL + u)
        return carry

    lax.fori_loop(0, count // UNROLL, trip, 0)
    for t in range(count // UNROLL * UNROLL, count):
        step(t)


def fold_rows(a):
    return jnp.max(a.reshape(B // 8, 8, B), axis=0)


def lane_peaks(acc, blocks, first, packed):
    lane = lax.broadcasted_iota(jnp.int32, (B, B), 1)
    for b in range(blocks):
        peak = jnp.max(acc[b], axis=1, keepdims=True)
        packed = jnp.where(lane == first + b, peak, packed)
    return packed


def spread_rows(rep, scales):
    n = scales.shape[0]
    turned = jnp.concatenate([scales, jnp.zeros((B - n, B), F32)], axis=0).T
    for b in range(n):
        rep[b] = jnp.broadcast_to(turned[:, b : b + 1], (B, B))


def col_peaks(acc, col_blocks):
    return jnp.concatenate(
        [jnp.max(acc[c], axis=0, keepdims=True) for c in range(col_blocks)], axis=0
    )


def first_peaks(rb, cb, slots, meta, tiles, peaks, scale_col, racc, cacc):
    racc[...] = jnp.zeros_like(racc)
    cacc[...] = jnp.zeros_like(cacc)

    def plain(t):
        a = jnp.abs(tiles[t].astype(F32))
        r, c = meta[t], meta[slots + t]
        racc[r] = jnp.maximum(racc[r], a)
        cacc[c] = jnp.maximum(cacc[c], fold_rows(a))

    loop(slots, plain)
    packed = lane_peaks(racc, rb, 0, jnp.zeros((B, B), F32))
    scale_col[0:cb] = 1.0 / jnp.sqrt(col_peaks(cacc, cb) + EPS)
    scale_col[cb : cb + 1] = jnp.zeros((1, B), F32)
    racc[...] = jnp.zeros_like(racc)

    def scaled(t):
        a = jnp.abs(tiles[t].astype(F32))
        r, c = meta[t], meta[slots + t]
        racc[r] = jnp.maximum(racc[r], a * scale_col[pl.ds(c, 1), :])

    loop(slots, scaled)
    packed = lane_peaks(racc, rb, rb, packed)
    peaks[...] = packed.T[0 : 2 * rb]


def second_peaks(rb, cb, slots, per, pays, meta, place, tiles, scale_col1, *refs):
    parts = refs[:pays]
    payload, scale_row2, scale_col3, dual = refs[pays : pays + 4]
    rep, cacc, dacc, scol2, scol3, racc, racc_b = refs[pays + 4 :]
    peak = parts[0][0 : 2 * rb]
    for p in parts[1:]:
        peak = jnp.maximum(peak, p[0 : 2 * rb])
    srow1 = 1.0 / jnp.sqrt(peak[0:rb] + EPS)
    srow2 = srow1 / jnp.sqrt(srow1 * peak[rb : 2 * rb] + EPS)
    scale_row2[...] = srow2
    spread_rows(rep, jnp.concatenate([srow1, srow2], axis=0))
    rep[2 * rb] = jnp.zeros((B, B), F32)
    for k, p in enumerate(parts):
        for i in range(per):
            dual[place[k] + i] = p[2 * rb + 32 * i : 2 * rb + 32 * (i + 1)]
    payload[2 * rb : 3 * rb] = jnp.concatenate(
        [jnp.sum(dual[b], axis=0, keepdims=True) for b in range(rb)], axis=0
    )
    cacc[...] = jnp.zeros_like(cacc)
    dacc[...] = jnp.zeros_like(dacc)

    def columns(t):
        a = jnp.abs(tiles[t].astype(F32))
        r, c = meta[t], meta[slots + t]
        s = jnp.minimum(r, rb - 1)
        cacc[c] = jnp.maximum(cacc[c], fold_rows(a * rep[s]))
        dacc[c] = jnp.maximum(dacc[c], fold_rows(a * rep[s + rb]))

    loop(slots, columns)
    c1 = scale_col1[0:cb]
    c2 = c1 / jnp.sqrt(c1 * col_peaks(cacc, cb) + EPS)
    c3 = c2 / jnp.sqrt(c2 * col_peaks(dacc, cb) + EPS)
    scol2[0:cb] = c2
    scol3[0:cb] = c3
    scol2[cb : cb + 1] = jnp.zeros((1, B), F32)
    scol3[cb : cb + 1] = jnp.zeros((1, B), F32)
    scale_col3[...] = c3
    racc[...] = jnp.zeros_like(racc)
    racc_b[...] = jnp.zeros_like(racc_b)

    def rows(t):
        a = jnp.abs(tiles[t].astype(F32))
        r, c = meta[t], meta[slots + t]
        racc[r] = jnp.maximum(racc[r], a * scol2[pl.ds(c, 1), :])
        racc_b[r] = jnp.maximum(racc_b[r], a * scol3[pl.ds(c, 1), :])

    loop(slots, rows)
    packed = lane_peaks(racc, rb, 0, jnp.zeros((B, B), F32))
    packed = lane_peaks(racc_b, rb, rb, packed)
    payload[0 : 2 * rb] = packed.T[0 : 2 * rb]


def stack_dual(low, mean):
    hi = mean.astype(BF16).astype(F32)
    mid = (mean - hi).astype(BF16).astype(F32)
    lo = mean - hi - mid
    at = lax.broadcasted_iota(jnp.int32, (16, B), 0)
    tail = jnp.where(at == 0, hi, jnp.where(at == 1, mid, jnp.where(at == 2, lo, 0.0)))
    return jnp.concatenate([low, tail.astype(BF16)], axis=0)


def iterate(
    rb, cb, slots, scen_all, meta, mat, lhs, gacc, lacc, mixed, offsets, scol, read_plan, read_hold, write
):
    gacc[...] = jnp.zeros_like(gacc)

    def pull(t):
        r, c = jnp.minimum(meta[t], rb - 1), jnp.minimum(meta[slots + t], cb - 1)
        gacc[c] += jnp.dot(lhs[r], mat[t], preferred_element_type=F32)

    loop(slots, pull)
    for c in range(cb):
        scale = scol[c : c + 1]
        off = offsets[c : c + 1].astype(F32)
        cost = COST_RATE * off * scale
        hold_cost = (HOLD_BASE + COST_RATE * off) * scale
        grad = gacc[c, 0:32]
        mean_grad = (gacc[c, 32:33] + gacc[c, 33:34] + gacc[c, 34:35]) / scen_all
        plan, hold = read_plan(c, scale), read_hold(c, scale)
        plan_next = jnp.clip(plan - TAU_PLAN * (cost + mean_grad), 0.0, 1.0 / scale)
        hold_next = jnp.clip(hold - TAU_HOLD * (hold_cost + grad), 0.0, HOLD_CAP / scale)
        mixed[c] = ((2.0 * plan_next - plan) + (2.0 * hold_next - hold)).astype(BF16)
        write(c, scale, plan_next, hold_next)
    lacc[...] = jnp.zeros_like(lacc)

    def push(t):
        r, c = jnp.minimum(meta[t], rb - 1), jnp.minimum(meta[slots + t], cb - 1)
        lacc[r] += lax.dot_general(
            mixed[c], mat[t], (((1,), (1,)), ((), ())), preferred_element_type=F32
        )

    loop(slots, push)


def first_step(rb, cb, slots, scen_all, pays, split, meta, *refs):
    tiles, scale_row2, scale_col3, dual, offsets, capacity, plan0, hold0 = refs[:8]
    parts = refs[8 : 8 + pays]
    refs = refs[8 + pays :]
    mat, scale_row4, scale_col4, plan1, hold1 = refs[:5]
    loads, refs = refs[5 : 7 if split else 6], refs[7 if split else 6 :]
    rep, cacc, lhs, gacc, lacc, mixed = refs
    me = meta[2 * slots]
    peak = parts[0][0 : 2 * rb]
    ysum = parts[0][2 * rb : 3 * rb]
    for p in parts[1:]:
        peak = jnp.maximum(peak, p[0 : 2 * rb])
        ysum = ysum + p[2 * rb : 3 * rb]
    srow2 = scale_row2[...]
    srow3 = srow2 / jnp.sqrt(srow2 * peak[0:rb] + EPS)
    srow4 = srow3 / jnp.sqrt(srow3 * peak[rb : 2 * rb] + EPS)
    scale_row4[...] = srow4
    spread_rows(rep, jnp.concatenate([srow3, srow4], axis=0))
    rep[2 * rb] = jnp.zeros((B, B), F32)
    cacc[...] = jnp.zeros_like(cacc)

    def columns(t):
        a = jnp.abs(tiles[t].astype(F32))
        r, c = meta[t], meta[slots + t]
        cacc[c] = jnp.maximum(cacc[c], fold_rows(a * rep[jnp.minimum(r, rb - 1)]))

    loop(slots, columns)
    c3 = scale_col3[...]
    scale_col4[...] = c3 / jnp.sqrt(c3 * col_peaks(cacc, cb) + EPS)

    def build(t):
        r, c = meta[t], jnp.minimum(meta[slots + t], cb - 1)
        mat[t] = (tiles[t].astype(F32) * rep[r + rb] * scale_col4[pl.ds(c, 1), :]).astype(BF16)

    loop(slots, build)
    ymean = ysum / srow4
    for b in range(rb):
        low = (dual[b] / srow4[b : b + 1]).astype(BF16)
        lhs[b] = stack_dual(low, ymean[b : b + 1])

    def write(c, scale, plan, hold):
        plan1[c : c + 1] = plan
        hold1[:, c * B : (c + 1) * B] = hold

    iterate(
        rb, cb, slots, scen_all, meta, mat, lhs, gacc, lacc, mixed, offsets, scale_col4,
        lambda c, scale: plan0[c : c + 1] / scale,
        lambda c, scale: hold0[:, c * B : (c + 1) * B] / scale,
        write,
    )
    own = scale_row4[pl.ds(me, 1), :]
    lacc[me] += dual[me] / own * (1.0 / SIGMA) - CAP_UNIT * capacity[...].astype(F32) * own
    if split:
        parity = lax.rem(me, 2)
        for j in range(rb // 2):
            loads[0][j] = lacc[2 * j + parity]
            loads[1][j] = lacc[2 * j + 1 - parity]
    else:
        loads[0][...] = lacc[...]


def last_step(rb, cb, slots, scen_all, groups, stride, means, meta, place, *refs):
    mat, own_row, scale_col4, offsets, capacity, plan1, hold1, own_dual = refs[:8]
    lows = refs[8 : 8 + groups]
    sums = refs[8 + groups : 8 + groups + means]
    plan2, hold2, load, lhs, gacc, mixed = refs[8 + groups + means :]
    me = meta[2 * slots]
    ymean = sums[0][...]
    for s in sums[1:]:
        ymean = ymean + s[...]
    per = rb // groups
    for k in range(groups):
        for i in range(per):
            at = k * per + i
            lhs[place[k] + stride * i] = stack_dual(lows[k][i], ymean[at : at + 1])

    def write(c, scale, plan, hold):
        plan2[c : c + 1] = plan * scale
        hold2[:, c * B : (c + 1) * B] = hold * scale

    iterate(
        rb, cb, slots, scen_all, meta, mat, lhs, gacc, load, mixed, offsets, scale_col4,
        lambda c, scale: plan1[c : c + 1],
        lambda c, scale: hold1[:, c * B : (c + 1) * B],
        write,
    )
    own = own_row[...]
    load[me] += own_dual[...] * (1.0 / SIGMA) - CAP_UNIT * capacity[...].astype(F32) * own


def flip(x, axis, mask):
    n = lax.axis_size(axis)
    return lax.ppermute(x, axis, [(i, i ^ mask) for i in range(n)])


def flip_both(x, flt_mask, scn_mask):
    nf, ns = lax.axis_size("flt"), lax.axis_size("scn")
    pairs = [
        (f * ns + s, (f ^ flt_mask) * ns + (s ^ scn_mask)) for f in range(nf) for s in range(ns)
    ]
    return lax.ppermute(x, ("flt", "scn"), pairs)


def body(tiles, tile_row, tile_col, tile_count, slot_offset, capacity, plan0, hold0, dual0):
    slots = tiles.shape[0]
    cb = plan0.shape[0] // B
    nf, ns = lax.axis_size("flt"), lax.axis_size("scn")
    scen = dual0.shape[0]
    rb = nf
    scen_all = scen * ns
    small = nf == 8 and ns == 4
    me = lax.axis_index("flt").astype(jnp.int32)
    chip, core = me // 2, me % 2
    live = jnp.arange(slots, dtype=jnp.int32) < tile_count[0]
    meta = jnp.concatenate(
        [jnp.where(live, tile_row, rb), jnp.where(live, tile_col, cb), me[None]]
    )
    offsets = slot_offset.reshape(cb, B)
    f32 = functools.partial(jax.ShapeDtypeStruct, dtype=F32)

    peaks, scol1 = call(
        functools.partial(first_peaks, rb, cb, slots),
        [f32((2 * rb, B)), f32((cb + 1, B))],
        [pltpu.VMEM((rb + 1, B, B), F32), pltpu.VMEM((cb + 1, 8, B), F32)],
        1,
        1,
    )(meta, tiles)
    if small:
        mine = jnp.concatenate([peaks, dual0], axis=0)
        other = flip(mine, "flt", 1)
        both = [jnp.where(core == 0, dual0, other[2 * rb :]), jnp.where(core == 0, other[2 * rb :], dual0)]
        mine = jnp.concatenate([jnp.maximum(peaks, other[: 2 * rb])] + both, axis=0)
        parts = [mine] + [flip(mine, "flt", 2 * m) for m in (1, 2, 3)]
        place = jnp.stack([2 * (chip ^ m) for m in range(4)])
        per = 2
    else:
        gathered = lax.all_gather(dual0, "flt", axis=0, tiled=True)
        parts = [jnp.concatenate([lax.pmax(peaks, "flt"), gathered], axis=0)]
        place = jnp.zeros((1,), jnp.int32)
        per = rb
    payload, srow2, scol3, dual = call(
        functools.partial(second_peaks, rb, cb, slots, per, len(parts)),
        [f32((3 * rb, B)), f32((rb, B)), f32((cb, B)), f32((rb, scen, B))],
        [
            pltpu.VMEM((2 * rb + 1, B, B), F32),
            pltpu.VMEM((cb + 1, 8, B), F32),
            pltpu.VMEM((cb + 1, 8, B), F32),
            pltpu.VMEM((cb + 1, B), F32),
            pltpu.VMEM((cb + 1, B), F32),
            pltpu.VMEM((rb + 1, B, B), F32),
            pltpu.VMEM((rb + 1, B, B), F32),
        ],
        2,
        2 + len(parts),
    )(meta, place, tiles, scol1, *parts)
    peaks, ysum = payload[: 2 * rb], payload[2 * rb :]
    if small:
        mine = jnp.concatenate([jnp.maximum(peaks, flip(peaks, "flt", 1)), ysum], axis=0)
        parts = [mine] + [flip_both(mine, 2 * m, m) for m in (1, 2, 3)]
    else:
        parts = [jnp.concatenate([lax.pmax(peaks, "flt"), lax.psum(ysum, "scn")], axis=0)]
    lhs = pltpu.VMEM((rb, 48, B), BF16)
    gacc = pltpu.VMEM((cb, 48, B), F32)
    mixed = pltpu.VMEM((cb, scen, B), BF16)
    halves = [f32((rb // 2, scen, B))] * 2 if small else [f32((rb, scen, B))]
    outs = call(
        functools.partial(first_step, rb, cb, slots, scen_all, len(parts), small),
        [
            jax.ShapeDtypeStruct((slots, B, B), BF16),
            f32((rb, B)),
            f32((cb, B)),
            f32((cb, B)),
            f32((scen, cb * B)),
        ]
        + halves,
        [
            pltpu.VMEM((2 * rb + 1, B, B), F32),
            pltpu.VMEM((cb + 1, 8, B), F32),
            lhs,
            gacc,
            pltpu.VMEM((rb, scen, B), F32),
            mixed,
        ],
        1,
        8 + len(parts),
    )(meta, tiles, srow2, scol3, dual, offsets, capacity, plan0.reshape(cb, B), hold0, *parts)
    mat, srow4, scol4, plan1, hold1 = outs[:5]
    if small:
        half = outs[5] + flip(outs[6], "flt", 1)
        far = [flip(half, "flt", 2 * m) for m in (1, 2, 3)]
        y = jnp.maximum(SIGMA * (half + far[0] + far[1] + far[2]), 0.0)
        low = y.astype(BF16)
        part = jnp.sum(low.astype(F32), axis=1)
        lows = [low, flip(low, "flt", 1)]
        sums = jnp.concatenate([part, flip(part, "flt", 1)], axis=0)
        sums = [sums] + [flip(sums, "scn", m) for m in (1, 2, 3)]
        place = jnp.stack([core, 1 - core])
        own_dual = lax.dynamic_index_in_dim(y, chip, 0, False)
        stride = 2
    else:
        y = jnp.maximum(SIGMA * lax.psum(outs[5], "flt"), 0.0)
        lows = [y.astype(BF16)]
        sums = [lax.psum(jnp.sum(lows[0].astype(F32), axis=1), "scn")]
        place = jnp.zeros((1,), jnp.int32)
        own_dual = lax.dynamic_index_in_dim(y, me, 0, False)
        stride = 1
    own_row = lax.dynamic_slice_in_dim(srow4, me, 1, 0)
    plan, hold, load = call(
        functools.partial(last_step, rb, cb, slots, scen_all, len(lows), stride, len(sums)),
        [f32((cb, B)), f32((scen, cb * B)), f32((rb, scen, B))],
        [lhs, gacc, mixed],
        2,
        8 + len(lows) + len(sums),
    )(meta, place, mat, own_row, scol4, offsets, capacity, plan1, hold1, own_dual, *lows, *sums)
    total = jnp.sum(lax.all_to_all(load, "flt", 0, 0), axis=0)
    dual = jnp.maximum(SIGMA * total, 0.0) * own_row
    return plan.reshape(-1), hold, dual


def solution(mesh):
    return jax.shard_map(
        body,
        mesh=mesh,
        in_specs=(
            P("flt", None, None),
            P("flt"),
            P("flt"),
            P("flt"),
            P("flt"),
            P("scn", "flt"),
            P("flt"),
            P("scn", "flt"),
            P("scn", "flt"),
        ),
        out_specs=(P("flt"), P("scn", "flt"), P("scn", "flt")),
        check_vma=False,
    )
```

```python
import functools

import jax
import jax.numpy as jnp
from jax import lax
from jax.experimental import pallas as pl
from jax.experimental.pallas import tpu as pltpu
from jax.sharding import PartitionSpec as P

EPS = 1e-06
COST_RATE = 1.0
HOLD_BASE = 1.0
HOLD_CAP = 2.0
CAP_UNIT = 4.0
TAU_PLAN = 0.2
TAU_HOLD = 0.02
SIGMA = 0.05

B = 128
UNROLL = 16
VMEM = pl.BlockSpec(memory_space=pltpu.VMEM)
HBM = pl.BlockSpec(memory_space=pltpu.HBM)
F32 = jnp.float32
BF16 = jnp.bfloat16


def call(body, out_shape, scratch, n_hbm, n_vmem, limit=24 * 1024 * 1024):
    return pl.pallas_call(
        body,
        out_shape=out_shape,
        in_specs=[HBM] * n_hbm + [VMEM] * n_vmem,
        out_specs=[VMEM] * len(out_shape),
        scratch_shapes=scratch,
        compiler_params=pltpu.CompilerParams(vmem_limit_bytes=limit),
    )


def loop(first, last, unroll, step):
    trips = (last - first) // unroll

    def trip(i, carry):
        for u in range(unroll):
            step(first + i * unroll + u)
        return carry

    if trips == 1:
        trip(0, 0)
    else:
        lax.fori_loop(0, trips, trip, 0)
    for t in range(first + trips * unroll, last):
        step(t)


def index_scratch(slots):
    return [
        pltpu.SMEM((slots,), jnp.int32),
        pltpu.SMEM((slots,), jnp.int32),
        pltpu.SMEM((1,), jnp.int32),
        pltpu.SemaphoreType.DMA((3,)),
    ]


def fetch_index(sources, held):
    sems = held[3]
    copies = [pltpu.make_async_copy(s, held[i], sems.at[i]) for i, s in enumerate(sources)]
    for c in copies:
        c.start()

    def wait():
        for c in copies:
            c.wait()

    return wait


def position(held, rb, cb, t):
    live = t < held[2][0]
    return jnp.where(live, held[0][t], rb), jnp.where(live, held[1][t], cb)


def fold_rows(a):
    return jnp.max(a.reshape(B // 8, 8, B), axis=0)


def lane_peaks(acc, blocks, first, packed):
    lane = lax.broadcasted_iota(jnp.int32, (B, B), 1)
    for b in range(blocks):
        peak = jnp.max(acc[b].astype(F32), axis=1, keepdims=True)
        packed = jnp.where(lane == first + b, peak, packed)
    return packed


def spread_rows(rep, scales):
    n = scales.shape[0]
    turned = jnp.concatenate([scales, jnp.zeros((B - n, B), F32)], axis=0).T
    for b in range(n):
        rep[b] = jnp.broadcast_to(turned[:, b : b + 1], (B, B))


def col_peaks(acc, col_blocks):
    return jnp.concatenate(
        [jnp.max(acc[c], axis=0, keepdims=True) for c in range(col_blocks)], axis=0
    )


def first_peaks(rb, cb, slots, chunk, *refs):
    index, tiles_hbm, dual_hbm, payload, scale_col = refs[:3], refs[3], refs[4], refs[5], refs[6]
    held, (tiles, racc16, cacc16, racc, sems, dual_sem) = refs[7:11], refs[11:]
    wait_index = fetch_index(index, held)
    copies = [
        pltpu.make_async_copy(
            tiles_hbm.at[pl.ds(i * chunk, chunk)], tiles.at[pl.ds(i * chunk, chunk)], sems.at[i]
        )
        for i in range(slots // chunk)
    ]
    for c in copies:
        c.start()
    dual_copy = pltpu.make_async_copy(dual_hbm, payload.at[pl.ds(2 * rb, dual_hbm.shape[0])], dual_sem)
    dual_copy.start()
    racc16[...] = jnp.zeros_like(racc16)
    cacc16[...] = jnp.zeros_like(cacc16)
    racc[...] = jnp.zeros_like(racc)
    wait_index()

    def plain(t):
        a = jnp.abs(tiles[t])
        r, c = position(held, rb, cb, t)
        racc16[r] = jnp.maximum(racc16[r], a)
        cacc16[c] = jnp.maximum(cacc16[c], jnp.max(a.reshape(B // 16, 16, B), axis=0))

    for i, c in enumerate(copies):
        c.wait()
        loop(i * chunk, (i + 1) * chunk, chunk, plain)
    col_peak = jnp.concatenate(
        [jnp.max(cacc16[c].astype(F32), axis=0, keepdims=True) for c in range(cb)], axis=0
    )
    scale_col[0:cb] = 1.0 / jnp.sqrt(col_peak + EPS)
    scale_col[cb : cb + 1] = jnp.zeros((1, B), F32)

    def scaled(t):
        a = jnp.abs(tiles[t].astype(F32))
        r, c = position(held, rb, cb, t)
        racc[r] = jnp.maximum(racc[r], a * scale_col[pl.ds(c, 1), :])

    loop(0, slots, UNROLL, scaled)
    packed = lane_peaks(racc16, rb, 0, jnp.zeros((B, B), F32))
    packed = lane_peaks(racc, rb, rb, packed)
    payload[0 : 2 * rb] = packed.T[0 : 2 * rb]
    dual_copy.wait()


def second_peaks(rb, cb, slots, pays, *refs):
    index, tiles, scale_col1, parts = refs[:3], refs[3], refs[4], refs[5 : 5 + pays]
    peaks, scale_row2, scale_col3, dual = refs[5 + pays : 9 + pays]
    held, refs = refs[9 + pays : 13 + pays], refs[13 + pays :]
    rep, cacc, dacc, scol2, scol3, racc, racc_b = refs
    wait_index = fetch_index(index, held)
    chip = lax.axis_index("flt") // 2
    peak = parts[0][0 : 2 * rb]
    for p in parts[1:]:
        peak = jnp.maximum(peak, p[0 : 2 * rb])
    srow1 = 1.0 / jnp.sqrt(peak[0:rb] + EPS)
    srow2 = srow1 / jnp.sqrt(srow1 * peak[rb : 2 * rb] + EPS)
    scale_row2[...] = srow2
    spread_rows(rep, jnp.concatenate([srow1, srow2], axis=0))
    scen = dual.shape[1]
    per = rb // pays
    for k, p in enumerate(parts):
        for i in range(per):
            at = i if pays == 1 else 2 * (chip ^ k) + i
            dual[at] = p[2 * rb + scen * i : 2 * rb + scen * (i + 1)]
    cacc[...] = jnp.zeros_like(cacc)
    dacc[...] = jnp.zeros_like(dacc)
    racc[...] = jnp.zeros_like(racc)
    racc_b[...] = jnp.zeros_like(racc_b)
    wait_index()

    def columns(t):
        a = jnp.abs(tiles[t].astype(F32))
        r, c = position(held, 0, cb, t)
        cacc[c] = jnp.maximum(cacc[c], fold_rows(a * rep[r]))
        dacc[c] = jnp.maximum(dacc[c], fold_rows(a * rep[r + rb]))

    loop(0, slots, UNROLL, columns)
    c1 = scale_col1[0:cb]
    c2 = c1 / jnp.sqrt(c1 * col_peaks(cacc, cb) + EPS)
    c3 = c2 / jnp.sqrt(c2 * col_peaks(dacc, cb) + EPS)
    scol2[0:cb] = c2
    scol3[0:cb] = c3
    scol2[cb : cb + 1] = jnp.zeros((1, B), F32)
    scol3[cb : cb + 1] = jnp.zeros((1, B), F32)
    scale_col3[...] = c3

    def rows(t):
        a = jnp.abs(tiles[t].astype(F32))
        r, c = position(held, rb, cb, t)
        racc[r] = jnp.maximum(racc[r], a * scol2[pl.ds(c, 1), :])
        racc_b[r] = jnp.maximum(racc_b[r], a * scol3[pl.ds(c, 1), :])

    loop(0, slots, UNROLL, rows)
    packed = lane_peaks(racc, rb, 0, jnp.zeros((B, B), F32))
    packed = lane_peaks(racc_b, rb, rb, packed)
    peaks[...] = packed.T[0 : 2 * rb]


def pull(slots, held, mat, lhs, gacc):
    gacc[...] = jnp.zeros_like(gacc)

    def step(t):
        gacc[held[1][t]] += jnp.dot(lhs[held[0][t]], mat[t], preferred_element_type=F32)

    loop(0, slots, slots, step)


def holds(cb, gacc, offsets, scol, read_hold, write):
    for c in range(cb):
        scale = scol[c : c + 1]
        hold_cost = (HOLD_BASE + COST_RATE * offsets[c : c + 1].astype(F32)) * scale
        hold = read_hold(c, scale)
        hold_next = jnp.clip(hold - TAU_HOLD * (hold_cost + gacc[c]), 0.0, HOLD_CAP / scale)
        write(c, scale, hold_next, 2.0 * hold_next - hold)


def build_step(rb, cb, slots, *refs):
    index, refs = refs[:3], refs[3:]
    tiles, srow3, srow4, scale_col3, low, offsets, hold0, mat, scale_col4, hold1, turn = refs[:11]
    held, (rep, cacc, scol, gacc) = refs[11:15], refs[15:]
    wait_index = fetch_index(index, held)
    spread_rows(rep, jnp.concatenate([srow3[...], srow4[...]], axis=0))
    cacc[...] = jnp.zeros_like(cacc)
    wait_index()

    def columns(t):
        a = jnp.abs(tiles[t].astype(F32))
        r, c = position(held, 0, cb, t)
        cacc[c] = jnp.maximum(cacc[c], fold_rows(a * rep[r]))

    loop(0, slots, UNROLL, columns)
    c3 = scale_col3[...]
    c4 = c3 / jnp.sqrt(c3 * col_peaks(cacc, cb) + EPS)
    scale_col4[...] = c4
    scol[0:cb] = c4

    def build(t):
        live = (t < held[2][0]).astype(F32)
        r, c = held[0][t], held[1][t]
        value = tiles[t].astype(F32) * live * rep[r + rb] * scol[pl.ds(c, 1), :]
        mat[t] = value.astype(BF16)

    loop(0, slots, UNROLL, build)
    pull(slots, held, mat, low, gacc)

    def write(c, scale, hold, double):
        hold1[:, c * B : (c + 1) * B] = hold
        turn[:, c * B : (c + 1) * B] = double

    holds(
        cb, gacc, offsets, scol, lambda c, scale: hold0[:, c * B : (c + 1) * B] / scale, write
    )


def hold_step(rb, cb, slots, groups, *refs):
    index, mat, scol, offsets, hold1, lows = refs[:3], refs[3], refs[4], refs[5], refs[6], refs[7 : 7 + groups]
    hold2, turn = refs[7 + groups : 9 + groups]
    held, (low, gacc) = refs[9 + groups : 13 + groups], refs[13 + groups :]
    wait_index = fetch_index(index, held)
    core = lax.rem(lax.axis_index("flt"), 2)
    for k in range(groups):
        for i in range(rb // groups):
            at = i if groups == 1 else 2 * i + (core if k == 0 else 1 - core)
            low[at] = lows[k][i]
    wait_index()
    pull(slots, held, mat, low, gacc)

    def write(c, scale, hold, double):
        hold2[:, c * B : (c + 1) * B] = hold * scale
        turn[:, c * B : (c + 1) * B] = double

    holds(cb, gacc, offsets, scol, lambda c, scale: hold1[:, c * B : (c + 1) * B], write)


def plan_step(rb, cb, slots, scen_all, means, order, split, last, *refs):
    index, refs = refs[:3], refs[3:]
    mat, srow4, scol, offsets, capacity, plan, turn, own_dual = refs[:8]
    sums, refs = refs[8 : 8 + means], refs[8 + means :]
    plan_next, loads, refs = refs[0], refs[1 : 1 + split], refs[1 + split :]
    held, (lhs, gacc, lacc, mixed) = refs[:4], refs[4:]
    wait_index = fetch_index(index, held)
    me = lax.axis_index("flt")
    core = lax.rem(me, 2)
    total = sums[0][...]
    for s in sums[1:]:
        total = total + s[...]
    half = rb // 2
    for b in range(rb):
        at = b if not order else (2 * b + core if b < half else 2 * (b - half) + 1 - core)
        lhs[at] = three_terms(total[b : b + 1])
    wait_index()
    pull(slots, held, mat, lhs, gacc)
    for c in range(cb):
        scale = scol[c : c + 1]
        cost = COST_RATE * offsets[c : c + 1].astype(F32) * scale
        mean_grad = (gacc[c, 0:1] + gacc[c, 1:2] + gacc[c, 2:3]) / scen_all
        x = plan[c : c + 1] if last else plan[c : c + 1] / scale
        x_next = jnp.clip(x - TAU_PLAN * (cost + mean_grad), 0.0, 1.0 / scale)
        mixed[c] = ((2.0 * x_next - x) + turn[:, c * B : (c + 1) * B]).astype(BF16)
        plan_next[c : c + 1] = x_next * scale if last else x_next
    lacc[...] = jnp.zeros_like(lacc)

    def push(t):
        lacc[held[0][t]] += lax.dot_general(
            mixed[held[1][t]], mat[t], (((1,), (1,)), ((), ())), preferred_element_type=F32
        )

    loop(0, slots, slots, push)
    own = srow4[pl.ds(me, 1), :]
    lacc[me] += own_dual[...] * (1.0 / SIGMA) - CAP_UNIT * capacity[...].astype(F32) * own
    if split == 2:
        for j in range(half):
            loads[0][j] = lacc[2 * j + core]
            loads[1][j] = lacc[2 * j + 1 - core]
    else:
        loads[0][...] = lacc[...]


def three_terms(value):
    hi = value.astype(BF16).astype(F32)
    mid = (value - hi).astype(BF16).astype(F32)
    lo = value - hi - mid
    at = lax.broadcasted_iota(jnp.int32, (16, B), 0)
    terms = jnp.where(at == 0, hi, jnp.where(at == 1, mid, jnp.where(at == 2, lo, 0.0)))
    return terms.astype(BF16)


def flip(x, axis, mask):
    n = lax.axis_size(axis)
    return lax.ppermute(x, axis, [(i, i ^ mask) for i in range(n)])


def in_hbm(x):
    return pltpu.with_memory_space_constraint(x, pltpu.HBM)


def scenario_sums(low):
    return jnp.sum(low.astype(F32), axis=1)


def body(tiles, tile_row, tile_col, tile_count, slot_offset, capacity, plan0, hold0, dual0):
    slots = tiles.shape[0]
    cb = plan0.shape[0] // B
    nf, ns = lax.axis_size("flt"), lax.axis_size("scn")
    scen = dual0.shape[0]
    rb = nf
    scen_all = scen * ns
    small = nf == 8 and ns == 4
    me = lax.axis_index("flt")
    chip, core = me // 2, me % 2
    index = (tile_row, tile_col, tile_count)
    offsets = slot_offset.reshape(cb, B)
    f32 = functools.partial(jax.ShapeDtypeStruct, dtype=F32)
    held = index_scratch(slots)
    chunk = 12 if slots % 12 == 0 else slots

    mine, scol1 = call(
        functools.partial(first_peaks, rb, cb, slots, chunk),
        [f32((2 * rb + scen, B)), f32((cb + 1, B))],
        held
        + [
            pltpu.VMEM((slots, B, B), BF16),
            pltpu.VMEM((rb + 1, B, B), BF16),
            pltpu.VMEM((cb + 1, 16, B), BF16),
            pltpu.VMEM((rb + 1, B, B), F32),
            pltpu.SemaphoreType.DMA((slots // chunk,)),
            pltpu.SemaphoreType.DMA,
        ],
        5,
        0,
    )(in_hbm(tile_row), in_hbm(tile_col), tile_count, in_hbm(tiles), in_hbm(dual0))
    n = 2 * rb
    if small:
        other = flip(mine, "flt", 1)
        even = jnp.where(core == 0, mine[n:], other[n:])
        odd = jnp.where(core == 0, other[n:], mine[n:])
        mine = jnp.concatenate([jnp.maximum(mine[:n], other[:n]), even, odd], axis=0)
        parts = [mine] + [flip(mine, "flt", 2 * m) for m in (1, 2, 3)]
    else:
        gathered = lax.all_gather(mine[n:], "flt", axis=0, tiled=True)
        parts = [jnp.concatenate([lax.pmax(mine[:n], "flt"), gathered], axis=0)]
    peaks, srow2, scol3, dual = call(
        functools.partial(second_peaks, rb, cb, slots, len(parts)),
        [f32((2 * rb, B)), f32((rb, B)), f32((cb, B)), f32((rb, scen, B))],
        held
        + [
            pltpu.VMEM((2 * rb, B, B), F32),
            pltpu.VMEM((cb + 1, 8, B), F32),
            pltpu.VMEM((cb + 1, 8, B), F32),
            pltpu.VMEM((cb + 1, B), F32),
            pltpu.VMEM((cb + 1, B), F32),
            pltpu.VMEM((rb + 1, B, B), F32),
            pltpu.VMEM((rb + 1, B, B), F32),
        ],
        3,
        2 + len(parts),
    )(*index, tiles, scol1, *parts)
    if small:
        mine = jnp.maximum(peaks, flip(peaks, "flt", 1))
        far = [flip(mine, "flt", 2 * m) for m in (1, 2, 3)]
        peak = jnp.maximum(jnp.maximum(mine, far[0]), jnp.maximum(far[1], far[2]))
    else:
        peak = lax.pmax(peaks, "flt")
    srow3 = srow2 / jnp.sqrt(srow2 * peak[:rb] + EPS)
    srow4 = srow3 / jnp.sqrt(srow3 * peak[rb:] + EPS)
    own_row = lax.dynamic_slice_in_dim(srow4, me, 1, 0)
    low = (dual / srow4[:, None, :]).astype(BF16)
    sums = scenario_sums(low)
    own_dual = dual0 / own_row
    gacc = pltpu.VMEM((cb, scen, B), F32)
    mat, scol4, hold1, turn = call(
        functools.partial(build_step, rb, cb, slots),
        [
            jax.ShapeDtypeStruct((slots, B, B), BF16),
            f32((cb, B)),
            f32((scen, cb * B)),
            f32((scen, cb * B)),
        ],
        held
        + [
            pltpu.VMEM((2 * rb, B, B), F32),
            pltpu.VMEM((cb + 1, 8, B), F32),
            pltpu.VMEM((cb, B), F32),
            gacc,
        ],
        3,
        7,
    )(*index, tiles, srow3, srow4, scol3, low, offsets, hold0)
    plan = plan0.reshape(cb, B)
    for step in range(2):
        if step:
            if small:
                half = loads[0] + flip(loads[1], "flt", 1)
                far = [flip(half, "flt", 2 * m) for m in (1, 2, 3)]
                y = jnp.maximum(SIGMA * (half + far[0] + far[1] + far[2]), 0.0)
                low = y.astype(BF16)
                part = scenario_sums(low)
                lows = [low, flip(low, "flt", 1)]
                sums = jnp.concatenate([part, flip(part, "flt", 1)], axis=0)
                own_dual = lax.dynamic_index_in_dim(y, chip, 0, False)
            else:
                y = jnp.maximum(SIGMA * lax.psum(loads[0], "flt"), 0.0)
                lows = [y.astype(BF16)]
                sums = scenario_sums(lows[0])
                own_dual = lax.dynamic_index_in_dim(y, me, 0, False)
            hold, turn = call(
                functools.partial(hold_step, rb, cb, slots, len(lows)),
                [f32((scen, cb * B)), f32((scen, cb * B))],
                held + [pltpu.VMEM((rb, scen, B), BF16), gacc],
                3,
                4 + len(lows),
            )(*index, mat, scol4, offsets, hold1, *lows)
        if small:
            totals = [sums] + [flip(sums, "scn", m) for m in (1, 2, 3)]
        else:
            totals = [lax.psum(sums, "scn")]
        split = 2 if small and not step else 1
        plan, *loads = call(
            functools.partial(
                plan_step, rb, cb, slots, scen_all, len(totals), small and step == 1, split, step == 1
            ),
            [f32((cb, B))] + [f32((rb // split, scen, B))] * split,
            held
            + [
                pltpu.VMEM((rb, 16, B), BF16),
                pltpu.VMEM((cb, 16, B), F32),
                pltpu.VMEM((rb, scen, B), F32),
                pltpu.VMEM((cb, scen, B), BF16),
            ],
            3,
            8 + len(totals),
        )(*index, mat, srow4, scol4, offsets, capacity, plan, turn, own_dual, *totals)
    total = jnp.sum(lax.all_to_all(loads[0], "flt", 0, 0), axis=0)
    dual = jnp.maximum(SIGMA * total, 0.0) * own_row
    return plan.reshape(-1), hold, dual


def solution(mesh):
    return jax.shard_map(
        body,
        mesh=mesh,
        in_specs=(
            P("flt", None, None),
            P("flt"),
            P("flt"),
            P("flt"),
            P("flt"),
            P("scn", "flt"),
            P("flt"),
            P("scn", "flt"),
            P("scn", "flt"),
        ),
        out_specs=(P("flt"), P("scn", "flt"), P("scn", "flt")),
        check_vma=False,
    )
```

```python
import functools

import jax
import jax.numpy as jnp
from jax import lax
from jax.experimental import pallas as pl
from jax.experimental.pallas import tpu as pltpu
from jax.sharding import PartitionSpec as P

EPS = 1e-06
COST_RATE = 1.0
HOLD_BASE = 1.0
HOLD_CAP = 2.0
CAP_UNIT = 4.0
TAU_PLAN = 0.2
TAU_HOLD = 0.02
SIGMA = 0.05

B = 128
UNROLL = 48
FIRST, SECOND = (2, 6), (4, 4)
FIRST_SCN, SECOND_SCN = (1, 3), (2, 2)
VMEM = pl.BlockSpec(memory_space=pltpu.VMEM)
HBM = pl.BlockSpec(memory_space=pltpu.HBM)
F32 = jnp.float32
BF16 = jnp.bfloat16


def call(body, out_shape, scratch, n_hbm, n_vmem, limit=24 * 1024 * 1024):
    return pl.pallas_call(
        body,
        out_shape=out_shape,
        in_specs=[HBM] * n_hbm + [VMEM] * n_vmem,
        out_specs=[VMEM] * len(out_shape),
        scratch_shapes=scratch,
        compiler_params=pltpu.CompilerParams(vmem_limit_bytes=limit),
    )


def loop(first, last, unroll, step):
    trips = (last - first) // unroll

    def trip(i, carry):
        for u in range(unroll):
            step(first + i * unroll + u)
        return carry

    if trips == 1:
        trip(0, 0)
    else:
        lax.fori_loop(0, trips, trip, 0)
    for t in range(first + trips * unroll, last):
        step(t)


def index_scratch(slots):
    return [
        pltpu.SMEM((slots,), jnp.int32),
        pltpu.SMEM((slots,), jnp.int32),
        pltpu.SMEM((1,), jnp.int32),
        pltpu.SemaphoreType.DMA((3,)),
    ]


def fetch_index(sources, held):
    sems = held[3]
    copies = [pltpu.make_async_copy(s, held[i], sems.at[i]) for i, s in enumerate(sources)]
    for c in copies:
        c.start()

    def wait():
        for c in copies:
            c.wait()

    return wait


def position(held, rb, cb, t):
    live = t < held[2][0]
    return jnp.where(live, held[0][t], rb), jnp.where(live, held[1][t], cb)


def fold_rows(a):
    return jnp.max(a.reshape(B // 8, 8, B), axis=0)


def lane_peaks(acc, blocks, first, packed):
    lane = lax.broadcasted_iota(jnp.int32, (B, B), 1)
    for b in range(blocks):
        peak = jnp.max(acc[b].astype(F32), axis=1, keepdims=True)
        packed = jnp.where(lane == first + b, peak, packed)
    return packed


def spread_rows(rep, scales):
    n = scales.shape[0]
    turned = jnp.concatenate([scales, jnp.zeros((B - n, B), F32)], axis=0).T
    for b in range(n):
        rep[b] = jnp.broadcast_to(turned[:, b : b + 1], (B, B))


def col_peaks(acc, col_blocks):
    return jnp.concatenate(
        [jnp.max(acc[c], axis=0, keepdims=True) for c in range(col_blocks)], axis=0
    )


def first_peaks(rb, cb, slots, chunk, *refs):
    index, tiles_hbm, dual_hbm, payload, scale_col = refs[:3], refs[3], refs[4], refs[5], refs[6]
    held, (tiles, racc16, cacc16, racc, sems, dual_sem) = refs[7:11], refs[11:]
    wait_index = fetch_index(index, held)
    copies = [
        pltpu.make_async_copy(
            tiles_hbm.at[pl.ds(i * chunk, chunk)], tiles.at[pl.ds(i * chunk, chunk)], sems.at[i]
        )
        for i in range(slots // chunk)
    ]
    for c in copies:
        c.start()
    dual_copy = pltpu.make_async_copy(dual_hbm, payload.at[pl.ds(2 * rb, dual_hbm.shape[0])], dual_sem)
    dual_copy.start()
    racc16[...] = jnp.zeros_like(racc16)
    cacc16[...] = jnp.zeros_like(cacc16)
    racc[...] = jnp.zeros_like(racc)
    wait_index()

    def plain(t):
        a = jnp.abs(tiles[t])
        r, c = position(held, rb, cb, t)
        racc16[r] = jnp.maximum(racc16[r], a)
        cacc16[c] = jnp.maximum(cacc16[c], jnp.max(a.reshape(B // 16, 16, B), axis=0))

    for i, c in enumerate(copies):
        c.wait()
        loop(i * chunk, (i + 1) * chunk, chunk, plain)
    col_peak = jnp.concatenate(
        [jnp.max(cacc16[c].astype(F32), axis=0, keepdims=True) for c in range(cb)], axis=0
    )
    scale_col[0:cb] = 1.0 / jnp.sqrt(col_peak + EPS)
    scale_col[cb : cb + 1] = jnp.zeros((1, B), F32)

    def scaled(t):
        a = jnp.abs(tiles[t].astype(F32))
        r, c = position(held, rb, cb, t)
        racc[r] = jnp.maximum(racc[r], a * scale_col[pl.ds(c, 1), :])

    loop(0, slots, UNROLL, scaled)
    packed = lane_peaks(racc16, rb, 0, jnp.zeros((B, B), F32))
    packed = lane_peaks(racc, rb, rb, packed)
    payload[0 : 2 * rb] = packed.T[0 : 2 * rb]
    dual_copy.wait()


def second_peaks(rb, cb, slots, pays, *refs):
    index, tiles, scale_col1, parts = refs[:3], refs[3], refs[4], refs[5 : 5 + pays]
    peaks, scale_row2, scale_col3, dual = refs[5 + pays : 9 + pays]
    held, refs = refs[9 + pays : 13 + pays], refs[13 + pays :]
    rep, cacc, dacc, scol2, scol3, racc, racc_b = refs
    wait_index = fetch_index(index, held)
    me = lax.axis_index("flt")
    chip, core = me // 2, lax.rem(me, 2)
    peak = parts[0][0 : 2 * rb]
    for p in parts[1:]:
        peak = jnp.maximum(peak, p[0 : 2 * rb])
    srow1 = 1.0 / jnp.sqrt(peak[0:rb] + EPS)
    srow2 = srow1 / jnp.sqrt(srow1 * peak[rb : 2 * rb] + EPS)
    scale_row2[...] = srow2
    spread_rows(rep, jnp.concatenate([srow1, srow2], axis=0))
    scen = dual.shape[1]
    n = 2 * rb
    if pays == 1:
        for i in range(rb):
            dual[i] = parts[0][n + scen * i : n + scen * (i + 1)]
    else:
        mine, first, second, other = [p[n:] for p in parts]
        got = [mine, jnp.where(core == 0, first, other), second, jnp.where(core == 0, other, first)]
        for k, g in enumerate(got):
            for i in range(2):
                dual[2 * (chip ^ k) + i] = g[scen * i : scen * (i + 1)]
    cacc[...] = jnp.zeros_like(cacc)
    dacc[...] = jnp.zeros_like(dacc)
    racc[...] = jnp.zeros_like(racc)
    racc_b[...] = jnp.zeros_like(racc_b)
    wait_index()

    def columns(t):
        a = jnp.abs(tiles[t].astype(F32))
        r, c = position(held, 0, cb, t)
        cacc[c] = jnp.maximum(cacc[c], fold_rows(a * rep[r]))
        dacc[c] = jnp.maximum(dacc[c], fold_rows(a * rep[r + rb]))

    loop(0, slots, UNROLL, columns)
    c1 = scale_col1[0:cb]
    c2 = c1 / jnp.sqrt(c1 * col_peaks(cacc, cb) + EPS)
    c3 = c2 / jnp.sqrt(c2 * col_peaks(dacc, cb) + EPS)
    scol2[0:cb] = c2
    scol3[0:cb] = c3
    scol2[cb : cb + 1] = jnp.zeros((1, B), F32)
    scol3[cb : cb + 1] = jnp.zeros((1, B), F32)
    scale_col3[...] = c3

    def rows(t):
        a = jnp.abs(tiles[t].astype(F32))
        r, c = position(held, rb, cb, t)
        racc[r] = jnp.maximum(racc[r], a * scol2[pl.ds(c, 1), :])
        racc_b[r] = jnp.maximum(racc_b[r], a * scol3[pl.ds(c, 1), :])

    loop(0, slots, UNROLL, rows)
    packed = lane_peaks(racc, rb, 0, jnp.zeros((B, B), F32))
    packed = lane_peaks(racc_b, rb, rb, packed)
    peaks[...] = packed.T[0 : 2 * rb]


def pull(slots, held, mat, lhs, gacc):
    gacc[...] = jnp.zeros_like(gacc)

    def step(t):
        gacc[held[1][t]] += jnp.dot(lhs[held[0][t]], mat[t], preferred_element_type=F32)

    loop(0, slots, slots, step)


def holds(cb, gacc, offsets, scol, read_hold, write):
    for c in range(cb):
        scale = scol[c : c + 1]
        hold_cost = (HOLD_BASE + COST_RATE * offsets[c : c + 1].astype(F32)) * scale
        hold = read_hold(c, scale)
        hold_next = jnp.clip(hold - TAU_HOLD * (hold_cost + gacc[c]), 0.0, HOLD_CAP / scale)
        write(c, scale, hold_next, 2.0 * hold_next - hold)


def build_step(rb, cb, slots, *refs):
    index, refs = refs[:3], refs[3:]
    tiles, srow3, srow4, scale_col3, low, offsets, hold0, mat, scale_col4, hold1, turn = refs[:11]
    held, (rep, cacc, scol, gacc) = refs[11:15], refs[15:]
    wait_index = fetch_index(index, held)
    spread_rows(rep, jnp.concatenate([srow3[...], srow4[...]], axis=0))
    cacc[...] = jnp.zeros_like(cacc)
    wait_index()

    def columns(t):
        a = jnp.abs(tiles[t].astype(F32))
        r, c = position(held, 0, cb, t)
        cacc[c] = jnp.maximum(cacc[c], fold_rows(a * rep[r]))

    loop(0, slots, UNROLL, columns)
    c3 = scale_col3[...]
    c4 = c3 / jnp.sqrt(c3 * col_peaks(cacc, cb) + EPS)
    scale_col4[...] = c4
    scol[0:cb] = c4

    def build(t):
        live = (t < held[2][0]).astype(F32)
        r, c = held[0][t], held[1][t]
        value = tiles[t].astype(F32) * live * rep[r + rb] * scol[pl.ds(c, 1), :]
        mat[t] = value.astype(BF16)

    loop(0, slots, UNROLL, build)
    pull(slots, held, mat, low, gacc)

    def write(c, scale, hold, double):
        hold1[:, c * B : (c + 1) * B] = hold
        turn[:, c * B : (c + 1) * B] = double

    holds(
        cb, gacc, offsets, scol, lambda c, scale: hold0[:, c * B : (c + 1) * B] / scale, write
    )


def hold_step(rb, cb, slots, *refs):
    index, (mat, scol, offsets, hold1, low), (hold2, turn) = refs[:3], refs[3:8], refs[8:10]
    held, gacc = refs[10:14], refs[14]
    fetch_index(index, held)()
    pull(slots, held, mat, low, gacc)

    def write(c, scale, hold, double):
        hold2[:, c * B : (c + 1) * B] = hold * scale
        turn[:, c * B : (c + 1) * B] = double

    holds(cb, gacc, offsets, scol, lambda c, scale: hold1[:, c * B : (c + 1) * B], write)


def plan_step(rb, cb, slots, scen_all, means, split, last, *refs):
    index, refs = refs[:3], refs[3:]
    mat, srow4, scol, offsets, capacity, plan, turn, own_dual = refs[:8]
    sums, refs = refs[8 : 8 + means], refs[8 + means :]
    plan_next, loads, refs = refs[0], refs[1 : 1 + split], refs[1 + split :]
    held, (lhs, gacc, lacc, mixed) = refs[:4], refs[4:]
    wait_index = fetch_index(index, held)
    me = lax.axis_index("flt")
    chip, core = me // 2, lax.rem(me, 2)
    total = sums[0][...]
    if means > 1:
        first, second, other = [s[...] for s in sums[1:]]
        total = (total + jnp.where(core == 0, first, other)) + (second + jnp.where(core == 0, other, first))
    for b in range(rb):
        lhs[b] = three_terms(total[b : b + 1])
    wait_index()
    pull(slots, held, mat, lhs, gacc)
    for c in range(cb):
        scale = scol[c : c + 1]
        cost = COST_RATE * offsets[c : c + 1].astype(F32) * scale
        mean_grad = (gacc[c, 0:1] + gacc[c, 1:2] + gacc[c, 2:3]) / scen_all
        x = plan[c : c + 1] if last else plan[c : c + 1] / scale
        x_next = jnp.clip(x - TAU_PLAN * (cost + mean_grad), 0.0, 1.0 / scale)
        mixed[c] = ((2.0 * x_next - x) + turn[:, c * B : (c + 1) * B]).astype(BF16)
        plan_next[c : c + 1] = x_next * scale if last else x_next
    lacc[...] = jnp.zeros_like(lacc)

    def push(t):
        lacc[held[0][t]] += lax.dot_general(
            mixed[held[1][t]], mat[t], (((1,), (1,)), ((), ())), preferred_element_type=F32
        )

    loop(0, slots, slots, push)
    own = srow4[pl.ds(me, 1), :]
    lacc[me] += own_dual[...] * (1.0 / SIGMA) - CAP_UNIT * capacity[...].astype(F32) * own
    if split == 2:
        for k, mine in enumerate((core, 1 - core)):
            via = chip ^ (1 + 2 * mine)
            if last:
                picks = (2 * chip + mine, 2 * via, 2 * via + 1, 2 * (chip ^ 2) + mine)
            else:
                picks = [2 * j + mine for j in range(rb // 2)]
            for j, b in enumerate(picks):
                loads[k][j] = lacc[b]
    else:
        loads[0][...] = lacc[...]


def three_terms(value):
    hi = value.astype(BF16).astype(F32)
    mid = (value - hi).astype(BF16).astype(F32)
    lo = value - hi - mid
    at = lax.broadcasted_iota(jnp.int32, (16, B), 0)
    terms = jnp.where(at == 0, hi, jnp.where(at == 1, mid, jnp.where(at == 2, lo, 0.0)))
    return terms.astype(BF16)


def cross(x, even, odd):
    pairs = [(i, i ^ (odd if i % 2 else even)) for i in range(lax.axis_size("flt"))]
    return lax.ppermute(x, "flt", pairs)


def cross_scn(x, even, odd):
    nf, ns = lax.axis_size("flt"), lax.axis_size("scn")
    pairs = [(f * ns + s, f * ns + (s ^ (odd if f % 2 else even))) for f in range(nf) for s in range(ns)]
    return lax.ppermute(x, ("flt", "scn"), pairs)


def twin(x):
    return lax.ppermute(x, "flt", [(i, i ^ 1) for i in range(lax.axis_size("flt"))])


def interleave(mine, other, core):
    even, odd = jnp.where(core == 0, mine, other), jnp.where(core == 0, other, mine)
    return jnp.stack([even, odd], axis=1).reshape((-1,) + mine.shape[1:])


def in_hbm(x):
    return pltpu.with_memory_space_constraint(x, pltpu.HBM)


def round_low(y):
    rounded = lax.reduce_precision(y, 8, 7)
    return rounded.astype(BF16), jnp.sum(rounded, axis=1)


def body(tiles, tile_row, tile_col, tile_count, slot_offset, capacity, plan0, hold0, dual0):
    slots = tiles.shape[0]
    cb = plan0.shape[0] // B
    nf, ns = lax.axis_size("flt"), lax.axis_size("scn")
    scen = dual0.shape[0]
    rb = nf
    scen_all = scen * ns
    small = nf == 8 and ns == 4
    me = lax.axis_index("flt")
    chip, core = me // 2, me % 2
    index = (tile_row, tile_col, tile_count)
    offsets = slot_offset.reshape(cb, B)
    f32 = functools.partial(jax.ShapeDtypeStruct, dtype=F32)
    held = index_scratch(slots)
    chunk = 12 if slots % 12 == 0 else slots

    mine, scol1 = call(
        functools.partial(first_peaks, rb, cb, slots, chunk),
        [f32((2 * rb + scen, B)), f32((cb + 1, B))],
        held
        + [
            pltpu.VMEM((slots, B, B), BF16),
            pltpu.VMEM((rb + 1, B, B), BF16),
            pltpu.VMEM((cb + 1, 16, B), BF16),
            pltpu.VMEM((rb + 1, B, B), F32),
            pltpu.SemaphoreType.DMA((slots // chunk,)),
            pltpu.SemaphoreType.DMA,
        ],
        5,
        0,
    )(in_hbm(tile_row), in_hbm(tile_col), tile_count, in_hbm(tiles), in_hbm(dual0))
    n = 2 * rb
    if small:
        other = twin(mine)
        even = jnp.where(core == 0, mine[n:], other[n:])
        odd = jnp.where(core == 0, other[n:], mine[n:])
        mine = jnp.concatenate([jnp.maximum(mine[:n], other[:n]), even, odd], axis=0)
        first, second = cross(mine, *FIRST), cross(mine, *SECOND)
        best = jnp.maximum(mine[:n], first[:n])
        parts = [mine, first, second, twin(jnp.concatenate([best, first[n:]], axis=0))]
    else:
        gathered = lax.all_gather(mine[n:], "flt", axis=0, tiled=True)
        parts = [jnp.concatenate([lax.pmax(mine[:n], "flt"), gathered], axis=0)]
    peaks, srow2, scol3, dual = call(
        functools.partial(second_peaks, rb, cb, slots, len(parts)),
        [f32((2 * rb, B)), f32((rb, B)), f32((cb, B)), f32((rb, scen, B))],
        held
        + [
            pltpu.VMEM((2 * rb, B, B), F32),
            pltpu.VMEM((cb + 1, 8, B), F32),
            pltpu.VMEM((cb + 1, 8, B), F32),
            pltpu.VMEM((cb + 1, B), F32),
            pltpu.VMEM((cb + 1, B), F32),
            pltpu.VMEM((rb + 1, B, B), F32),
            pltpu.VMEM((rb + 1, B, B), F32),
        ],
        3,
        2 + len(parts),
    )(*index, tiles, scol1, *parts)
    if small:
        mine = jnp.maximum(peaks, twin(peaks))
        best, second = jnp.maximum(mine, cross(mine, *FIRST)), cross(mine, *SECOND)
        peak = jnp.maximum(jnp.maximum(best, second), twin(best))
    else:
        peak = lax.pmax(peaks, "flt")
    srow3 = srow2 / jnp.sqrt(srow2 * peak[:rb] + EPS)
    srow4 = srow3 / jnp.sqrt(srow3 * peak[rb:] + EPS)
    own_row = lax.dynamic_slice_in_dim(srow4, me, 1, 0)
    low, sums = round_low(dual / srow4[:, None, :])
    own_dual = dual0 / own_row
    gacc = pltpu.VMEM((cb, scen, B), F32)
    mat, scol4, hold1, turn = call(
        functools.partial(build_step, rb, cb, slots),
        [
            jax.ShapeDtypeStruct((slots, B, B), BF16),
            f32((cb, B)),
            f32((scen, cb * B)),
            f32((scen, cb * B)),
        ],
        held
        + [
            pltpu.VMEM((2 * rb, B, B), F32),
            pltpu.VMEM((cb + 1, 8, B), F32),
            pltpu.VMEM((cb, B), F32),
            gacc,
        ],
        3,
        7,
    )(*index, tiles, srow3, srow4, scol3, low, offsets, hold0)
    plan = plan0.reshape(cb, B)
    for step in range(2):
        if step:
            if small:
                half = loads[0] + twin(loads[1])
                far = [cross(half, m, m) for m in (2, 4, 6)]
                y = jnp.maximum(SIGMA * ((half + far[0]) + (far[1] + far[2])), 0.0)
                low, sums = round_low(y)
                low, sums = interleave(low, twin(low), core), interleave(sums, twin(sums), core)
                own_dual = lax.dynamic_index_in_dim(y, chip, 0, False)
            else:
                y = jnp.maximum(SIGMA * lax.psum(loads[0], "flt"), 0.0)
                low, sums = round_low(y)
                own_dual = lax.dynamic_index_in_dim(y, me, 0, False)
            hold, turn = call(
                functools.partial(hold_step, rb, cb, slots),
                [f32((scen, cb * B)), f32((scen, cb * B))],
                held + [gacc],
                3,
                5,
            )(*index, mat, scol4, offsets, hold1, low)
        if small:
            first, second = cross_scn(sums, *FIRST_SCN), cross_scn(sums, *SECOND_SCN)
            first, second, turn = lax.optimization_barrier((first, second, turn))
            totals = [sums, first, second, twin(first)]
        else:
            totals = [lax.psum(sums, "scn")]
        split = 2 if small else 1
        plan, *loads = call(
            functools.partial(
                plan_step, rb, cb, slots, scen_all, len(totals), split, step == 1
            ),
            [f32((cb, B))] + [f32((rb // split, scen, B))] * split,
            held
            + [
                pltpu.VMEM((rb, 16, B), BF16),
                pltpu.VMEM((cb, 16, B), F32),
                pltpu.VMEM((rb, scen, B), F32),
                pltpu.VMEM((cb, scen, B), BF16),
            ],
            3,
            8 + len(totals),
        )(*index, mat, srow4, scol4, offsets, capacity, plan, turn, own_dual, *totals)
    if small:
        chip_sum = loads[0] + twin(loads[1])
        first, second = cross(chip_sum[1:3], *FIRST), cross(chip_sum[3], *SECOND)
        own, other = [lax.dynamic_index_in_dim(first, i, 0, False) for i in (core, 1 - core)]
        total = (chip_sum[0] + own) + (second + twin(other))
    else:
        total = lax.psum_scatter(loads[0], "flt", scatter_dimension=0, tiled=False)
    dual = jnp.maximum(SIGMA * total, 0.0) * own_row
    return plan.reshape(-1), hold, dual


def solution(mesh):
    return jax.shard_map(
        body,
        mesh=mesh,
        in_specs=(
            P("flt", None, None),
            P("flt"),
            P("flt"),
            P("flt"),
            P("flt"),
            P("scn", "flt"),
            P("flt"),
            P("scn", "flt"),
            P("scn", "flt"),
        ),
        out_specs=(P("flt"), P("scn", "flt"), P("scn", "flt")),
        check_vma=False,
    )
```

```python
import functools

import jax
import jax.numpy as jnp
from jax import lax
from jax.experimental import pallas as pl
from jax.experimental.pallas import tpu as pltpu
from jax.sharding import PartitionSpec as P

EPS = 1e-06
COST_RATE = 1.0
HOLD_BASE = 1.0
HOLD_CAP = 2.0
CAP_UNIT = 4.0
TAU_PLAN = 0.2
TAU_HOLD = 0.02
SIGMA = 0.05

B = 128
UNROLL = 48
FIRST, SECOND = (2, 6), (4, 4)
FIRST_SCN, SECOND_SCN = (1, 3), (2, 2)
VMEM = pl.BlockSpec(memory_space=pltpu.VMEM)
HBM = pl.BlockSpec(memory_space=pltpu.HBM)
F32 = jnp.float32
BF16 = jnp.bfloat16


def call(body, out_shape, scratch, in_specs, limit=24 * 1024 * 1024):
    return pl.pallas_call(
        body,
        out_shape=out_shape,
        in_specs=in_specs,
        out_specs=[VMEM] * len(out_shape),
        scratch_shapes=scratch,
        compiler_params=pltpu.CompilerParams(vmem_limit_bytes=limit),
    )


def loop(first, last, unroll, step):
    trips = (last - first) // unroll

    def trip(i, carry):
        for u in range(unroll):
            step(first + i * unroll + u)
        return carry

    if trips == 1:
        trip(0, 0)
    else:
        lax.fori_loop(0, trips, trip, 0)
    for t in range(first + trips * unroll, last):
        step(t)


def read_codes(codes, held):
    row = codes[0:1, :]
    for t in range(held.shape[0]):
        held[t] = row[0, t]


def position(held, t):
    code = held[t]
    return code & 255, (code >> 8) & 255


def given(held, t):
    code = held[t]
    return (code >> 16) & 255, code >> 24


def fold_rows(a):
    return jnp.max(a.reshape(B // 8, 8, B), axis=0)


def lane_peaks(acc, blocks, first, packed):
    lane = lax.broadcasted_iota(jnp.int32, (B, B), 1)
    for b in range(blocks):
        peak = jnp.max(acc[b].astype(F32), axis=1, keepdims=True)
        packed = jnp.where(lane == first + b, peak, packed)
    return packed


def spread_rows(rep, scales):
    n = scales.shape[0]
    turned = jnp.concatenate([scales, jnp.zeros((B - n, B), F32)], axis=0).T
    for b in range(n):
        rep[b] = jnp.broadcast_to(turned[:, b : b + 1], (B, B))


def col_peaks(acc, col_blocks):
    return jnp.concatenate(
        [jnp.max(acc[c], axis=0, keepdims=True) for c in range(col_blocks)], axis=0
    )


def first_peaks(rb, cb, slots, chunk, *refs):
    count, row_hbm, col_hbm, tiles_hbm, dual_hbm = refs[:5]
    payload, scale_col, codes = refs[5:8]
    row, col, held, tiles, racc16, cacc16, racc, sems, index_sems, dual_sem = refs[8:]
    index_copies = [
        pltpu.make_async_copy(row_hbm, row, index_sems.at[0]),
        pltpu.make_async_copy(col_hbm, col, index_sems.at[1]),
    ]
    copies = [
        pltpu.make_async_copy(
            tiles_hbm.at[pl.ds(i * chunk, chunk)], tiles.at[pl.ds(i * chunk, chunk)], sems.at[i]
        )
        for i in range(slots // chunk)
    ]
    dual_copy = pltpu.make_async_copy(dual_hbm, payload.at[pl.ds(2 * rb, dual_hbm.shape[0])], dual_sem)
    for c in index_copies + copies + [dual_copy]:
        c.start()
    racc16[...] = jnp.zeros_like(racc16)
    cacc16[...] = jnp.zeros_like(cacc16)
    racc[...] = jnp.zeros_like(racc)
    for c in index_copies:
        c.wait()
    lane = lax.broadcasted_iota(jnp.int32, codes.shape, 1)
    packed = jnp.zeros(codes.shape, jnp.int32)
    for t in range(slots):
        r, c = row[t], col[t]
        code = jnp.where(t < count[0], r + (c << 8), rb + (cb << 8)) + (r << 16) + (c << 24)
        held[t] = code
        packed = jnp.where(lane == t, code, packed)
    codes[...] = packed

    def plain(t):
        a = jnp.abs(tiles[t])
        r, c = position(held, t)
        racc16[r] = jnp.maximum(racc16[r], a)
        cacc16[c] = jnp.maximum(cacc16[c], jnp.max(a.reshape(B // 16, 16, B), axis=0))

    for i, c in enumerate(copies):
        c.wait()
        loop(i * chunk, (i + 1) * chunk, chunk, plain)
    col_peak = jnp.concatenate(
        [jnp.max(cacc16[c].astype(F32), axis=0, keepdims=True) for c in range(cb)], axis=0
    )
    scale_col[0:cb] = 1.0 / jnp.sqrt(col_peak + EPS)
    scale_col[cb : cb + 1] = jnp.zeros((1, B), F32)

    def scaled(t):
        a = jnp.abs(tiles[t].astype(F32))
        r, c = position(held, t)
        racc[r] = jnp.maximum(racc[r], a * scale_col[pl.ds(c, 1), :])

    loop(0, slots, UNROLL, scaled)
    packed = lane_peaks(racc16, rb, 0, jnp.zeros((B, B), F32))
    packed = lane_peaks(racc, rb, rb, packed)
    payload[0 : 2 * rb] = packed.T[0 : 2 * rb]
    dual_copy.wait()


def second_peaks(rb, cb, slots, pays, *refs):
    codes, tiles, scale_col1, parts = refs[0], refs[1], refs[2], refs[3 : 3 + pays]
    peaks, scale_row2, scale_col3, dual = refs[3 + pays : 7 + pays]
    held, rep, cacc, dacc, scol2, scol3, racc, racc_b = refs[7 + pays :]
    read_codes(codes, held)
    me = lax.axis_index("flt")
    chip, core = me // 2, lax.rem(me, 2)
    peak = parts[0][0 : 2 * rb]
    for p in parts[1:]:
        peak = jnp.maximum(peak, p[0 : 2 * rb])
    srow1 = 1.0 / jnp.sqrt(peak[0:rb] + EPS)
    srow2 = srow1 / jnp.sqrt(srow1 * peak[rb : 2 * rb] + EPS)
    scale_row2[...] = srow2
    spread_rows(rep, jnp.concatenate([srow1, srow2], axis=0))
    scen = dual.shape[1]
    n = 2 * rb
    if pays == 1:
        for i in range(rb):
            dual[i] = parts[0][n + scen * i : n + scen * (i + 1)]
    else:
        mine, first, second, other = [p[n:] for p in parts]
        got = [mine, jnp.where(core == 0, first, other), second, jnp.where(core == 0, other, first)]
        for k, g in enumerate(got):
            for i in range(2):
                dual[2 * (chip ^ k) + i] = g[scen * i : scen * (i + 1)]
    cacc[...] = jnp.zeros_like(cacc)
    dacc[...] = jnp.zeros_like(dacc)
    racc[...] = jnp.zeros_like(racc)
    racc_b[...] = jnp.zeros_like(racc_b)

    def columns(t):
        a = jnp.abs(tiles[t].astype(F32))
        r, c = given(held, t)[0], position(held, t)[1]
        cacc[c] = jnp.maximum(cacc[c], fold_rows(a * rep[r]))
        dacc[c] = jnp.maximum(dacc[c], fold_rows(a * rep[r + rb]))

    loop(0, slots, UNROLL, columns)
    c1 = scale_col1[0:cb]
    c2 = c1 / jnp.sqrt(c1 * col_peaks(cacc, cb) + EPS)
    c3 = c2 / jnp.sqrt(c2 * col_peaks(dacc, cb) + EPS)
    scol2[0:cb] = c2
    scol3[0:cb] = c3
    scol2[cb : cb + 1] = jnp.zeros((1, B), F32)
    scol3[cb : cb + 1] = jnp.zeros((1, B), F32)
    scale_col3[...] = c3

    def rows(t):
        a = jnp.abs(tiles[t].astype(F32))
        r, c = position(held, t)
        racc[r] = jnp.maximum(racc[r], a * scol2[pl.ds(c, 1), :])
        racc_b[r] = jnp.maximum(racc_b[r], a * scol3[pl.ds(c, 1), :])

    loop(0, slots, UNROLL, rows)
    packed = lane_peaks(racc, rb, 0, jnp.zeros((B, B), F32))
    packed = lane_peaks(racc_b, rb, rb, packed)
    peaks[...] = packed.T[0 : 2 * rb]


def pull(slots, held, mat, lhs, gacc):
    gacc[...] = jnp.zeros_like(gacc)

    def step(t):
        r, c = given(held, t)
        gacc[c] += jnp.dot(lhs[r], mat[t], preferred_element_type=F32)

    loop(0, slots, slots, step)


def holds(cb, gacc, offsets, scol, read_hold, write):
    for c in range(cb):
        scale = scol[c : c + 1]
        hold_cost = (HOLD_BASE + COST_RATE * offsets[c : c + 1].astype(F32)) * scale
        hold = read_hold(c, scale)
        hold_next = jnp.clip(hold - TAU_HOLD * (hold_cost + gacc[c]), 0.0, HOLD_CAP / scale)
        write(c, scale, hold_next, 2.0 * hold_next - hold)


def build_step(rb, cb, slots, *refs):
    codes, tiles, srow3, srow4, scale_col3, low, offsets, hold0 = refs[:8]
    mat, scale_col4, hold1, turn, held, rep, cacc, scol, gacc = refs[8:]
    read_codes(codes, held)
    spread_rows(rep, jnp.concatenate([srow3[...], srow4[...]], axis=0))
    cacc[...] = jnp.zeros_like(cacc)

    def columns(t):
        a = jnp.abs(tiles[t].astype(F32))
        r, c = given(held, t)[0], position(held, t)[1]
        cacc[c] = jnp.maximum(cacc[c], fold_rows(a * rep[r]))

    loop(0, slots, UNROLL, columns)
    c3 = scale_col3[...]
    c4 = c3 / jnp.sqrt(c3 * col_peaks(cacc, cb) + EPS)
    scale_col4[...] = c4
    scol[0:cb] = c4

    def build(t):
        r, c = given(held, t)
        live = (position(held, t)[0] < rb).astype(F32)
        value = tiles[t].astype(F32) * live * rep[r + rb] * scol[pl.ds(c, 1), :]
        mat[t] = value.astype(BF16)

    loop(0, slots, UNROLL, build)
    pull(slots, held, mat, low, gacc)

    def write(c, scale, hold, double):
        hold1[:, c * B : (c + 1) * B] = hold
        turn[:, c * B : (c + 1) * B] = double

    holds(
        cb, gacc, offsets, scol, lambda c, scale: hold0[:, c * B : (c + 1) * B] / scale, write
    )


def hold_step(rb, cb, slots, *refs):
    codes, mat, scol, offsets, hold1, low, hold2, turn, held, gacc = refs
    read_codes(codes, held)
    pull(slots, held, mat, low, gacc)

    def write(c, scale, hold, double):
        hold2[:, c * B : (c + 1) * B] = hold * scale
        turn[:, c * B : (c + 1) * B] = double

    holds(cb, gacc, offsets, scol, lambda c, scale: hold1[:, c * B : (c + 1) * B], write)


def plan_step(rb, cb, slots, scen_all, means, split, last, *refs):
    codes, mat, srow4, scol, offsets, capacity, plan, turn, own_dual = refs[:9]
    sums, refs = refs[9 : 9 + means], refs[9 + means :]
    plan_next, loads = refs[0], refs[1 : 1 + split]
    held, lhs, gacc, lacc, mixed = refs[1 + split :]
    read_codes(codes, held)
    me = lax.axis_index("flt")
    chip, core = me // 2, lax.rem(me, 2)
    total = sums[0][...]
    if means > 1:
        first, second, other = [s[...] for s in sums[1:]]
        total = (total + jnp.where(core == 0, first, other)) + (second + jnp.where(core == 0, other, first))
    for b in range(rb):
        lhs[b] = three_terms(total[b : b + 1])
    pull(slots, held, mat, lhs, gacc)
    for c in range(cb):
        scale = scol[c : c + 1]
        cost = COST_RATE * offsets[c : c + 1].astype(F32) * scale
        mean_grad = (gacc[c, 0:1] + gacc[c, 1:2] + gacc[c, 2:3]) / scen_all
        x = plan[c : c + 1] if last else plan[c : c + 1] / scale
        x_next = jnp.clip(x - TAU_PLAN * (cost + mean_grad), 0.0, 1.0 / scale)
        mixed[c] = ((2.0 * x_next - x) + turn[:, c * B : (c + 1) * B]).astype(BF16)
        plan_next[c : c + 1] = x_next
    lacc[...] = jnp.zeros_like(lacc)

    def push(t):
        r, c = given(held, t)
        lacc[r] += lax.dot_general(
            mixed[c], mat[t], (((1,), (1,)), ((), ())), preferred_element_type=F32
        )

    loop(0, slots, slots, push)
    own = srow4[pl.ds(me, 1), :]
    lacc[me] += own_dual[...] * (1.0 / SIGMA) - CAP_UNIT * capacity[...].astype(F32) * own
    if split == 2:
        for k, mine in enumerate((core, 1 - core)):
            via = chip ^ (1 + 2 * mine)
            if last:
                picks = (2 * chip + mine, 2 * via, 2 * via + 1, 2 * (chip ^ 2) + mine)
            else:
                picks = [2 * j + mine for j in range(rb // 2)]
            for j, b in enumerate(picks):
                loads[k][j] = lacc[b]
    else:
        loads[0][...] = lacc[...]


def three_terms(value):
    hi = value.astype(BF16).astype(F32)
    mid = (value - hi).astype(BF16).astype(F32)
    lo = value - hi - mid
    at = lax.broadcasted_iota(jnp.int32, (16, B), 0)
    terms = jnp.where(at == 0, hi, jnp.where(at == 1, mid, jnp.where(at == 2, lo, 0.0)))
    return terms.astype(BF16)


def cross(x, even, odd):
    pairs = [(i, i ^ (odd if i % 2 else even)) for i in range(lax.axis_size("flt"))]
    return lax.ppermute(x, "flt", pairs)


def cross_scn(x, even, odd):
    nf, ns = lax.axis_size("flt"), lax.axis_size("scn")
    pairs = [(f * ns + s, f * ns + (s ^ (odd if f % 2 else even))) for f in range(nf) for s in range(ns)]
    return lax.ppermute(x, ("flt", "scn"), pairs)


def twin(x):
    return lax.ppermute(x, "flt", [(i, i ^ 1) for i in range(lax.axis_size("flt"))])


def interleave(mine, other, core):
    even, odd = jnp.where(core == 0, mine, other), jnp.where(core == 0, other, mine)
    return jnp.stack([even, odd], axis=1).reshape((-1,) + mine.shape[1:])


def in_hbm(x):
    return pltpu.with_memory_space_constraint(x, pltpu.HBM)


def round_low(y):
    rounded = lax.reduce_precision(y, 8, 7)
    return rounded.astype(BF16), jnp.sum(rounded, axis=1)


def body(tiles, tile_row, tile_col, tile_count, slot_offset, capacity, plan0, hold0, dual0):
    slots = tiles.shape[0]
    cb = plan0.shape[0] // B
    nf, ns = lax.axis_size("flt"), lax.axis_size("scn")
    scen = dual0.shape[0]
    rb = nf
    scen_all = scen * ns
    small = nf == 8 and ns == 4
    me = lax.axis_index("flt")
    chip, core = me // 2, me % 2
    offsets = slot_offset.reshape(cb, B)
    f32 = functools.partial(jax.ShapeDtypeStruct, dtype=F32)
    held = [pltpu.SMEM((slots,), jnp.int32)]
    chunk = 12 if slots % 12 == 0 else slots

    mine, scol1, codes = call(
        functools.partial(first_peaks, rb, cb, slots, chunk),
        [f32((2 * rb + scen, B)), f32((cb + 1, B)), jax.ShapeDtypeStruct((8, B), jnp.int32)],
        held * 3
        + [
            pltpu.VMEM((slots, B, B), BF16),
            pltpu.VMEM((rb + 1, B, B), BF16),
            pltpu.VMEM((cb + 1, 16, B), BF16),
            pltpu.VMEM((rb + 1, B, B), F32),
            pltpu.SemaphoreType.DMA((slots // chunk,)),
            pltpu.SemaphoreType.DMA((2,)),
            pltpu.SemaphoreType.DMA,
        ],
        [pl.BlockSpec(memory_space=pltpu.SMEM)] + [HBM] * 4,
    )(tile_count, in_hbm(tile_row), in_hbm(tile_col), in_hbm(tiles), in_hbm(dual0))
    n = 2 * rb
    if small:
        other = twin(mine)
        even = jnp.where(core == 0, mine[n:], other[n:])
        odd = jnp.where(core == 0, other[n:], mine[n:])
        mine = jnp.concatenate([jnp.maximum(mine[:n], other[:n]), even, odd], axis=0)
        first, second = cross(mine, *FIRST), cross(mine, *SECOND)
        best = jnp.maximum(mine[:n], first[:n])
        parts = [mine, first, second, twin(jnp.concatenate([best, first[n:]], axis=0))]
    else:
        gathered = lax.all_gather(mine[n:], "flt", axis=0, tiled=True)
        parts = [jnp.concatenate([lax.pmax(mine[:n], "flt"), gathered], axis=0)]
    peaks, srow2, scol3, dual = call(
        functools.partial(second_peaks, rb, cb, slots, len(parts)),
        [f32((2 * rb, B)), f32((rb, B)), f32((cb, B)), f32((rb, scen, B))],
        held
        + [
            pltpu.VMEM((2 * rb, B, B), F32),
            pltpu.VMEM((cb + 1, 8, B), F32),
            pltpu.VMEM((cb + 1, 8, B), F32),
            pltpu.VMEM((cb + 1, B), F32),
            pltpu.VMEM((cb + 1, B), F32),
            pltpu.VMEM((rb + 1, B, B), F32),
            pltpu.VMEM((rb + 1, B, B), F32),
        ],
        [VMEM] * (3 + len(parts)),
    )(codes, tiles, scol1, *parts)
    if small:
        mine = jnp.maximum(peaks, twin(peaks))
        best, second = jnp.maximum(mine, cross(mine, *FIRST)), cross(mine, *SECOND)
        peak = jnp.maximum(jnp.maximum(best, second), twin(best))
    else:
        peak = lax.pmax(peaks, "flt")
    srow3 = srow2 / jnp.sqrt(srow2 * peak[:rb] + EPS)
    srow4 = srow3 / jnp.sqrt(srow3 * peak[rb:] + EPS)
    own_row = lax.dynamic_slice_in_dim(srow4, me, 1, 0)
    low, sums = round_low(dual / srow4[:, None, :])
    own_dual = dual0 / own_row
    gacc = pltpu.VMEM((cb, scen, B), F32)
    mat, scol4, hold1, turn = call(
        functools.partial(build_step, rb, cb, slots),
        [
            jax.ShapeDtypeStruct((slots, B, B), BF16),
            f32((cb, B)),
            f32((scen, cb * B)),
            f32((scen, cb * B)),
        ],
        held
        + [
            pltpu.VMEM((2 * rb, B, B), F32),
            pltpu.VMEM((cb + 1, 8, B), F32),
            pltpu.VMEM((cb, B), F32),
            gacc,
        ],
        [VMEM] * 8,
    )(codes, tiles, srow3, srow4, scol3, low, offsets, hold0)
    plan = plan0.reshape(cb, B)
    for step in range(2):
        if step:
            if small:
                half = loads[0] + twin(loads[1])
                far = [cross(half, m, m) for m in (2, 4, 6)]
                y = jnp.maximum(SIGMA * ((half + far[0]) + (far[1] + far[2])), 0.0)
                low, sums = round_low(y)
                low, sums = interleave(low, twin(low), core), interleave(sums, twin(sums), core)
                own_dual = lax.dynamic_index_in_dim(y, chip, 0, False)
            else:
                y = jnp.maximum(SIGMA * lax.psum(loads[0], "flt"), 0.0)
                low, sums = round_low(y)
                own_dual = lax.dynamic_index_in_dim(y, me, 0, False)
            hold, turn = call(
                functools.partial(hold_step, rb, cb, slots),
                [f32((scen, cb * B)), f32((scen, cb * B))],
                held + [gacc],
                [VMEM] * 6,
            )(codes, mat, scol4, offsets, hold1, low)
        if small:
            first, second = cross_scn(sums, *FIRST_SCN), cross_scn(sums, *SECOND_SCN)
            first, second, turn = lax.optimization_barrier((first, second, turn))
            totals = [sums, first, second, twin(first)]
        else:
            totals = [lax.psum(sums, "scn")]
        split = 2 if small else 1
        plan, *loads = call(
            functools.partial(
                plan_step, rb, cb, slots, scen_all, len(totals), split, step == 1
            ),
            [f32((cb, B))] + [f32((rb // split, scen, B))] * split,
            held
            + [
                pltpu.VMEM((rb, 16, B), BF16),
                pltpu.VMEM((cb, 16, B), F32),
                pltpu.VMEM((rb, scen, B), F32),
                pltpu.VMEM((cb, scen, B), BF16),
            ],
            [VMEM] * (9 + len(totals)),
        )(codes, mat, srow4, scol4, offsets, capacity, plan, turn, own_dual, *totals)
    if small:
        chip_sum = loads[0] + twin(loads[1])
        first, second = cross(chip_sum[1:3], *FIRST), cross(chip_sum[3], *SECOND)
        own, other = [lax.dynamic_index_in_dim(first, i, 0, False) for i in (core, 1 - core)]
        total = (chip_sum[0] + own) + (second + twin(other))
    else:
        total = lax.psum_scatter(loads[0], "flt", scatter_dimension=0, tiled=False)
    dual = jnp.maximum(SIGMA * total, 0.0) * own_row
    return (plan * scol4).reshape(-1), hold, dual


def solution(mesh):
    return jax.shard_map(
        body,
        mesh=mesh,
        in_specs=(
            P("flt", None, None),
            P("flt"),
            P("flt"),
            P("flt"),
            P("flt"),
            P("scn", "flt"),
            P("flt"),
            P("scn", "flt"),
            P("scn", "flt"),
        ),
        out_specs=(P("flt"), P("scn", "flt"), P("scn", "flt")),
        check_vma=False,
    )
```

```python
import functools

import jax
import jax.numpy as jnp
from jax import lax
from jax.experimental import pallas as pl
from jax.experimental.pallas import tpu as pltpu
from jax.sharding import PartitionSpec as P

EPS = 1e-06
COST_RATE = 1.0
HOLD_BASE = 1.0
HOLD_CAP = 2.0
CAP_UNIT = 4.0
TAU_PLAN = 0.2
TAU_HOLD = 0.02
SIGMA = 0.05

B = 128
UNROLL = 48
FIRST, SECOND = (2, 6), (4, 4)
FIRST_SCN, SECOND_SCN = (1, 3), (2, 2)
VMEM = pl.BlockSpec(memory_space=pltpu.VMEM)
HBM = pl.BlockSpec(memory_space=pltpu.HBM)
F32 = jnp.float32
BF16 = jnp.bfloat16


def call(body, out_shape, scratch, in_specs, limit=24 * 1024 * 1024):
    return pl.pallas_call(
        body,
        out_shape=out_shape,
        in_specs=in_specs,
        out_specs=[VMEM] * len(out_shape),
        scratch_shapes=scratch,
        compiler_params=pltpu.CompilerParams(vmem_limit_bytes=limit),
    )


def loop(first, last, unroll, step):
    trips = (last - first) // unroll

    def trip(i, carry):
        for u in range(unroll):
            step(first + i * unroll + u)
        return carry

    if trips == 1:
        trip(0, 0)
    else:
        lax.fori_loop(0, trips, trip, 0)
    for t in range(first + trips * unroll, last):
        step(t)


def read_codes(codes, held):
    row = codes[0:1, :]
    for t in range(held.shape[0]):
        held[t] = row[0, t]


def position(held, t):
    code = held[t]
    return code & 255, (code >> 8) & 255


def given(held, t):
    code = held[t]
    return (code >> 16) & 255, code >> 24


def fold_rows(a):
    return jnp.max(a.reshape(B // 8, 8, B), axis=0)


def lane_peaks(acc, blocks, first, packed):
    lane = lax.broadcasted_iota(jnp.int32, (B, B), 1)
    for b in range(blocks):
        peak = jnp.max(acc[b].astype(F32), axis=1, keepdims=True)
        packed = jnp.where(lane == first + b, peak, packed)
    return packed


def spread_rows(rep, scales):
    n = scales.shape[0]
    turned = jnp.concatenate([scales, jnp.zeros((B - n, B), F32)], axis=0).T
    for b in range(n):
        rep[b] = jnp.broadcast_to(turned[:, b : b + 1], (B, B))


def col_peaks(acc, col_blocks):
    return jnp.concatenate(
        [jnp.max(acc[c], axis=0, keepdims=True) for c in range(col_blocks)], axis=0
    )


def first_peaks(rb, cb, slots, chunk, *refs):
    count, row_hbm, col_hbm, tiles_hbm, dual_hbm = refs[:5]
    payload, scale_col, codes = refs[5:8]
    row, col, held, tiles, racc16, cacc16, racc, sems, index_sems, dual_sem = refs[8:]
    index_copies = [
        pltpu.make_async_copy(row_hbm, row, index_sems.at[0]),
        pltpu.make_async_copy(col_hbm, col, index_sems.at[1]),
    ]
    copies = [
        pltpu.make_async_copy(
            tiles_hbm.at[pl.ds(i * chunk, chunk)], tiles.at[pl.ds(i * chunk, chunk)], sems.at[i]
        )
        for i in range(slots // chunk)
    ]
    dual_copy = pltpu.make_async_copy(dual_hbm, payload.at[pl.ds(2 * rb, dual_hbm.shape[0])], dual_sem)
    for c in index_copies + copies + [dual_copy]:
        c.start()
    racc16[...] = jnp.zeros_like(racc16)
    cacc16[...] = jnp.zeros_like(cacc16)
    racc[...] = jnp.zeros_like(racc)
    for c in index_copies:
        c.wait()
    lane = lax.broadcasted_iota(jnp.int32, codes.shape, 1)
    packed = jnp.zeros(codes.shape, jnp.int32)
    for t in range(slots):
        r, c = row[t], col[t]
        code = jnp.where(t < count[0], r + (c << 8), rb + (cb << 8)) + (r << 16) + (c << 24)
        held[t] = code
        packed = jnp.where(lane == t, code, packed)
    codes[...] = packed

    def plain(t):
        a = jnp.abs(tiles[t])
        r, c = position(held, t)
        racc16[r] = jnp.maximum(racc16[r], a)
        cacc16[c] = jnp.maximum(cacc16[c], jnp.max(a.reshape(B // 16, 16, B), axis=0))

    for i, c in enumerate(copies):
        c.wait()
        loop(i * chunk, (i + 1) * chunk, chunk, plain)
    col_peak = jnp.concatenate(
        [jnp.max(cacc16[c].astype(F32), axis=0, keepdims=True) for c in range(cb)], axis=0
    )
    scale_col[0:cb] = 1.0 / jnp.sqrt(col_peak + EPS)
    scale_col[cb : cb + 1] = jnp.zeros((1, B), F32)

    def scaled(t):
        a = jnp.abs(tiles[t].astype(F32))
        r, c = position(held, t)
        racc[r] = jnp.maximum(racc[r], a * scale_col[pl.ds(c, 1), :])

    loop(0, slots, UNROLL, scaled)
    packed = lane_peaks(racc16, rb, 0, jnp.zeros((B, B), F32))
    packed = lane_peaks(racc, rb, rb, packed)
    payload[0 : 2 * rb] = packed.T[0 : 2 * rb]
    dual_copy.wait()


def second_peaks(rb, cb, slots, pays, *refs):
    codes, tiles, scale_col1, parts = refs[0], refs[1], refs[2], refs[3 : 3 + pays]
    peaks, scale_row2, scale_col3, dual = refs[3 + pays : 7 + pays]
    held, rep, cacc, dacc, scol2, scol3, racc, racc_b = refs[7 + pays :]
    read_codes(codes, held)
    me = lax.axis_index("flt")
    chip, core = me // 2, lax.rem(me, 2)
    peak = parts[0][0 : 2 * rb]
    for p in parts[1:]:
        peak = jnp.maximum(peak, p[0 : 2 * rb])
    srow1 = 1.0 / jnp.sqrt(peak[0:rb] + EPS)
    srow2 = srow1 / jnp.sqrt(srow1 * peak[rb : 2 * rb] + EPS)
    scale_row2[...] = srow2
    spread_rows(rep, jnp.concatenate([srow1, srow2], axis=0))
    scen = dual.shape[1]
    n = 2 * rb
    if pays == 1:
        for i in range(rb):
            dual[i] = parts[0][n + scen * i : n + scen * (i + 1)]
    else:
        mine, first, second, other = [p[n:] for p in parts]
        got = [mine, jnp.where(core == 0, first, other), second, jnp.where(core == 0, other, first)]
        for k, g in enumerate(got):
            for i in range(2):
                dual[2 * (chip ^ k) + i] = g[scen * i : scen * (i + 1)]
    cacc[...] = jnp.zeros_like(cacc)
    dacc[...] = jnp.zeros_like(dacc)
    racc[...] = jnp.zeros_like(racc)
    racc_b[...] = jnp.zeros_like(racc_b)

    def columns(t):
        a = jnp.abs(tiles[t].astype(F32))
        r, c = given(held, t)[0], position(held, t)[1]
        cacc[c] = jnp.maximum(cacc[c], fold_rows(a * rep[r]))
        dacc[c] = jnp.maximum(dacc[c], fold_rows(a * rep[r + rb]))

    loop(0, slots, 24, columns)
    c1 = scale_col1[0:cb]
    c2 = c1 / jnp.sqrt(c1 * col_peaks(cacc, cb) + EPS)
    c3 = c2 / jnp.sqrt(c2 * col_peaks(dacc, cb) + EPS)
    scol2[0:cb] = c2
    scol3[0:cb] = c3
    scol2[cb : cb + 1] = jnp.zeros((1, B), F32)
    scol3[cb : cb + 1] = jnp.zeros((1, B), F32)
    scale_col3[...] = c3

    def rows(t):
        a = jnp.abs(tiles[t].astype(F32))
        r, c = position(held, t)
        racc[r] = jnp.maximum(racc[r], a * scol2[pl.ds(c, 1), :])
        racc_b[r] = jnp.maximum(racc_b[r], a * scol3[pl.ds(c, 1), :])

    loop(0, slots, 24, rows)
    packed = lane_peaks(racc, rb, 0, jnp.zeros((B, B), F32))
    packed = lane_peaks(racc_b, rb, rb, packed)
    peaks[...] = packed.T[0 : 2 * rb]


def pull(slots, held, mat, lhs, gacc):
    gacc[...] = jnp.zeros_like(gacc)

    def step(t):
        r, c = given(held, t)
        gacc[c] += jnp.dot(lhs[r], mat[t], preferred_element_type=F32)

    loop(0, slots, slots, step)


def holds(cb, gacc, offsets, scol, read_hold, write):
    for c in range(cb):
        scale = scol[c : c + 1]
        hold_cost = (HOLD_BASE + COST_RATE * offsets[c : c + 1].astype(F32)) * scale
        hold = read_hold(c, scale)
        hold_next = jnp.clip(hold - TAU_HOLD * (hold_cost + gacc[c]), 0.0, HOLD_CAP / scale)
        write(c, scale, hold_next, 2.0 * hold_next - hold)


def build_step(rb, cb, slots, *refs):
    codes, tiles, srow3, srow4, scale_col3, low, offsets, hold0 = refs[:8]
    mat, scale_col4, hold1, turn, held, rep, cacc, scol, gacc = refs[8:]
    read_codes(codes, held)
    spread_rows(rep, jnp.concatenate([srow3[...], srow4[...]], axis=0))
    cacc[...] = jnp.zeros_like(cacc)

    def columns(t):
        a = jnp.abs(tiles[t].astype(F32))
        r, c = given(held, t)[0], position(held, t)[1]
        cacc[c] = jnp.maximum(cacc[c], fold_rows(a * rep[r]))

    loop(0, slots, UNROLL, columns)
    c3 = scale_col3[...]
    c4 = c3 / jnp.sqrt(c3 * col_peaks(cacc, cb) + EPS)
    scale_col4[...] = c4
    scol[0:cb] = c4

    def build(t):
        r, c = given(held, t)
        live = (position(held, t)[0] < rb).astype(F32)
        value = tiles[t].astype(F32) * live * rep[r + rb] * scol[pl.ds(c, 1), :]
        mat[t] = value.astype(BF16)

    loop(0, slots, UNROLL, build)
    pull(slots, held, mat, low, gacc)

    def write(c, scale, hold, double):
        hold1[:, c * B : (c + 1) * B] = hold
        turn[:, c * B : (c + 1) * B] = double

    holds(
        cb, gacc, offsets, scol, lambda c, scale: hold0[:, c * B : (c + 1) * B] / scale, write
    )


def hold_step(rb, cb, slots, *refs):
    codes, mat, scol, offsets, hold1, low, hold2, turn, held, gacc = refs
    read_codes(codes, held)
    pull(slots, held, mat, low, gacc)

    def write(c, scale, hold, double):
        hold2[:, c * B : (c + 1) * B] = hold * scale
        turn[:, c * B : (c + 1) * B] = double

    holds(cb, gacc, offsets, scol, lambda c, scale: hold1[:, c * B : (c + 1) * B], write)


def plan_step(rb, cb, slots, scen_all, means, split, last, *refs):
    codes, mat, srow4, scol, offsets, capacity, plan, turn, own_dual = refs[:9]
    sums, refs = refs[9 : 9 + means], refs[9 + means :]
    plan_next, loads = refs[0], refs[1 : 1 + split]
    held, lhs, gacc, lacc, mixed = refs[1 + split :]
    read_codes(codes, held)
    me = lax.axis_index("flt")
    chip, core = me // 2, lax.rem(me, 2)
    total = sums[0][...]
    if means > 1:
        first, second, other = [s[...] for s in sums[1:]]
        total = (total + jnp.where(core == 0, first, other)) + (second + jnp.where(core == 0, other, first))
    for b in range(rb):
        lhs[b] = three_terms(total[b : b + 1])
    pull(slots, held, mat, lhs, gacc)
    for c in range(cb):
        scale = scol[c : c + 1]
        cost = COST_RATE * offsets[c : c + 1].astype(F32) * scale
        mean_grad = (gacc[c, 0:1] + gacc[c, 1:2] + gacc[c, 2:3]) / scen_all
        x = plan[c : c + 1] if last else plan[c : c + 1] / scale
        x_next = jnp.clip(x - TAU_PLAN * (cost + mean_grad), 0.0, 1.0 / scale)
        mixed[c] = ((2.0 * x_next - x) + turn[:, c * B : (c + 1) * B]).astype(BF16)
        plan_next[c : c + 1] = x_next
    lacc[...] = jnp.zeros_like(lacc)

    def push(t):
        r, c = given(held, t)
        lacc[r] += lax.dot_general(
            mixed[c], mat[t], (((1,), (1,)), ((), ())), preferred_element_type=F32
        )

    loop(0, slots, slots, push)
    own = srow4[pl.ds(me, 1), :]
    lacc[me] += own_dual[...] * (1.0 / SIGMA) - CAP_UNIT * capacity[...].astype(F32) * own
    if split == 2:
        for k, mine in enumerate((core, 1 - core)):
            via = chip ^ (1 + 2 * mine)
            if last:
                picks = (2 * chip + mine, 2 * via, 2 * via + 1, 2 * (chip ^ 2) + mine)
            else:
                picks = [2 * j + mine for j in range(rb // 2)]
            for j, b in enumerate(picks):
                loads[k][j] = lacc[b]
    else:
        loads[0][...] = lacc[...]


def three_terms(value):
    hi = value.astype(BF16).astype(F32)
    mid = (value - hi).astype(BF16).astype(F32)
    lo = value - hi - mid
    at = lax.broadcasted_iota(jnp.int32, (16, B), 0)
    terms = jnp.where(at == 0, hi, jnp.where(at == 1, mid, jnp.where(at == 2, lo, 0.0)))
    return terms.astype(BF16)


def cross(x, even, odd):
    pairs = [(i, i ^ (odd if i % 2 else even)) for i in range(lax.axis_size("flt"))]
    return lax.ppermute(x, "flt", pairs)


def cross_scn(x, even, odd):
    nf, ns = lax.axis_size("flt"), lax.axis_size("scn")
    pairs = [(f * ns + s, f * ns + (s ^ (odd if f % 2 else even))) for f in range(nf) for s in range(ns)]
    return lax.ppermute(x, ("flt", "scn"), pairs)


def twin(x):
    return lax.ppermute(x, "flt", [(i, i ^ 1) for i in range(lax.axis_size("flt"))])


def interleave(mine, other, core):
    even, odd = jnp.where(core == 0, mine, other), jnp.where(core == 0, other, mine)
    return jnp.stack([even, odd], axis=1).reshape((-1,) + mine.shape[1:])


def in_hbm(x):
    return pltpu.with_memory_space_constraint(x, pltpu.HBM)


def round_low(y):
    rounded = lax.reduce_precision(y, 8, 7)
    return rounded.astype(BF16), jnp.sum(rounded, axis=1)


def body(tiles, tile_row, tile_col, tile_count, slot_offset, capacity, plan0, hold0, dual0):
    slots = tiles.shape[0]
    cb = plan0.shape[0] // B
    nf, ns = lax.axis_size("flt"), lax.axis_size("scn")
    scen = dual0.shape[0]
    rb = nf
    scen_all = scen * ns
    small = nf == 8 and ns == 4
    me = lax.axis_index("flt")
    chip, core = me // 2, me % 2
    offsets = slot_offset.reshape(cb, B)
    f32 = functools.partial(jax.ShapeDtypeStruct, dtype=F32)
    held = [pltpu.SMEM((slots,), jnp.int32)]
    chunk = 12 if slots % 12 == 0 else slots

    mine, scol1, codes = call(
        functools.partial(first_peaks, rb, cb, slots, chunk),
        [f32((2 * rb + scen, B)), f32((cb + 1, B)), jax.ShapeDtypeStruct((8, B), jnp.int32)],
        held * 3
        + [
            pltpu.VMEM((slots, B, B), BF16),
            pltpu.VMEM((rb + 1, B, B), BF16),
            pltpu.VMEM((cb + 1, 16, B), BF16),
            pltpu.VMEM((rb + 1, B, B), F32),
            pltpu.SemaphoreType.DMA((slots // chunk,)),
            pltpu.SemaphoreType.DMA((2,)),
            pltpu.SemaphoreType.DMA,
        ],
        [pl.BlockSpec(memory_space=pltpu.SMEM)] + [HBM] * 4,
    )(tile_count, in_hbm(tile_row), in_hbm(tile_col), in_hbm(tiles), in_hbm(dual0))
    n = 2 * rb
    if small:
        other = twin(mine)
        even = jnp.where(core == 0, mine[n:], other[n:])
        odd = jnp.where(core == 0, other[n:], mine[n:])
        mine = jnp.concatenate([jnp.maximum(mine[:n], other[:n]), even, odd], axis=0)
        first, second = cross(mine, *FIRST), cross(mine, *SECOND)
        best = jnp.maximum(mine[:n], first[:n])
        parts = [mine, first, second, twin(jnp.concatenate([best, first[n:]], axis=0))]
    else:
        gathered = lax.all_gather(mine[n:], "flt", axis=0, tiled=True)
        parts = [jnp.concatenate([lax.pmax(mine[:n], "flt"), gathered], axis=0)]
    peaks, srow2, scol3, dual = call(
        functools.partial(second_peaks, rb, cb, slots, len(parts)),
        [f32((2 * rb, B)), f32((rb, B)), f32((cb, B)), f32((rb, scen, B))],
        held
        + [
            pltpu.VMEM((2 * rb, B, B), F32),
            pltpu.VMEM((cb + 1, 8, B), F32),
            pltpu.VMEM((cb + 1, 8, B), F32),
            pltpu.VMEM((cb + 1, B), F32),
            pltpu.VMEM((cb + 1, B), F32),
            pltpu.VMEM((rb + 1, B, B), F32),
            pltpu.VMEM((rb + 1, B, B), F32),
        ],
        [VMEM] * (3 + len(parts)),
    )(codes, tiles, scol1, *parts)
    if small:
        mine = jnp.maximum(peaks, twin(peaks))
        best, second = jnp.maximum(mine, cross(mine, *FIRST)), cross(mine, *SECOND)
        peak = jnp.maximum(jnp.maximum(best, second), twin(best))
    else:
        peak = lax.pmax(peaks, "flt")
    srow3 = srow2 / jnp.sqrt(srow2 * peak[:rb] + EPS)
    srow4 = srow3 / jnp.sqrt(srow3 * peak[rb:] + EPS)
    own_row = lax.dynamic_slice_in_dim(srow4, me, 1, 0)
    low, sums = round_low(dual / srow4[:, None, :])
    own_dual = dual0 / own_row
    gacc = pltpu.VMEM((cb, scen, B), F32)
    mat, scol4, hold1, turn = call(
        functools.partial(build_step, rb, cb, slots),
        [
            jax.ShapeDtypeStruct((slots, B, B), BF16),
            f32((cb, B)),
            f32((scen, cb * B)),
            f32((scen, cb * B)),
        ],
        held
        + [
            pltpu.VMEM((2 * rb, B, B), F32),
            pltpu.VMEM((cb + 1, 8, B), F32),
            pltpu.VMEM((cb, B), F32),
            gacc,
        ],
        [VMEM] * 8,
    )(codes, tiles, srow3, srow4, scol3, low, offsets, hold0)
    plan = plan0.reshape(cb, B)
    for step in range(2):
        if step:
            if small:
                half = loads[0] + twin(loads[1])
                far = [cross(half, m, m) for m in (2, 4, 6)]
                y = jnp.maximum(SIGMA * ((half + far[0]) + (far[1] + far[2])), 0.0)
                low, sums = round_low(y)
                low, sums = interleave(low, twin(low), core), interleave(sums, twin(sums), core)
                own_dual = lax.dynamic_index_in_dim(y, chip, 0, False)
            else:
                y = jnp.maximum(SIGMA * lax.psum(loads[0], "flt"), 0.0)
                low, sums = round_low(y)
                own_dual = lax.dynamic_index_in_dim(y, me, 0, False)
            hold, turn = call(
                functools.partial(hold_step, rb, cb, slots),
                [f32((scen, cb * B)), f32((scen, cb * B))],
                held + [gacc],
                [VMEM] * 6,
            )(codes, mat, scol4, offsets, hold1, low)
        if small:
            first, second = cross_scn(sums, *FIRST_SCN), cross_scn(sums, *SECOND_SCN)
            first, second, turn = lax.optimization_barrier((first, second, turn))
            totals = [sums, first, second, twin(first)]
        else:
            totals = [lax.psum(sums, "scn")]
        split = 2 if small else 1
        plan, *loads = call(
            functools.partial(
                plan_step, rb, cb, slots, scen_all, len(totals), split, step == 1
            ),
            [f32((cb, B))] + [f32((rb // split, scen, B))] * split,
            held
            + [
                pltpu.VMEM((rb, 16, B), BF16),
                pltpu.VMEM((cb, 16, B), F32),
                pltpu.VMEM((rb, scen, B), F32),
                pltpu.VMEM((cb, scen, B), BF16),
            ],
            [VMEM] * (9 + len(totals)),
        )(codes, mat, srow4, scol4, offsets, capacity, plan, turn, own_dual, *totals)
    if small:
        chip_sum = loads[0] + twin(loads[1])
        first, second = cross(chip_sum[1:3], *FIRST), cross(chip_sum[3], *SECOND)
        own, other = [lax.dynamic_index_in_dim(first, i, 0, False) for i in (core, 1 - core)]
        total = (chip_sum[0] + own) + (second + twin(other))
    else:
        total = lax.psum_scatter(loads[0], "flt", scatter_dimension=0, tiled=False)
    dual = jnp.maximum(SIGMA * total, 0.0) * own_row
    return (plan * scol4).reshape(-1), hold, dual


def solution(mesh):
    return jax.shard_map(
        body,
        mesh=mesh,
        in_specs=(
            P("flt", None, None),
            P("flt"),
            P("flt"),
            P("flt"),
            P("flt"),
            P("scn", "flt"),
            P("flt"),
            P("scn", "flt"),
            P("scn", "flt"),
        ),
        out_specs=(P("flt"), P("scn", "flt"), P("scn", "flt")),
        check_vma=False,
    )
```

```python
import functools

import jax
import jax.numpy as jnp
from jax import lax
from jax.experimental import pallas as pl
from jax.experimental.pallas import tpu as pltpu
from jax.sharding import PartitionSpec as P

EPS = 1e-06
COST_RATE = 1.0
HOLD_BASE = 1.0
HOLD_CAP = 2.0
CAP_UNIT = 4.0
TAU_PLAN = 0.2
TAU_HOLD = 0.02
SIGMA = 0.05

B = 128
UNROLL = 48
FIRST, SECOND = (2, 6), (4, 4)
FIRST_SCN, SECOND_SCN = (1, 3), (2, 2)
VMEM = pl.BlockSpec(memory_space=pltpu.VMEM)
HBM = pl.BlockSpec(memory_space=pltpu.HBM)
F32 = jnp.float32
BF16 = jnp.bfloat16


def call(body, out_shape, scratch, in_specs, limit=24 * 1024 * 1024):
    return pl.pallas_call(
        body,
        out_shape=out_shape,
        in_specs=in_specs,
        out_specs=[VMEM] * len(out_shape),
        scratch_shapes=scratch,
        compiler_params=pltpu.CompilerParams(vmem_limit_bytes=limit),
    )


def loop(first, last, unroll, step):
    trips = (last - first) // unroll

    def trip(i, carry):
        for u in range(unroll):
            step(first + i * unroll + u)
        return carry

    if trips == 1:
        trip(0, 0)
    else:
        lax.fori_loop(0, trips, trip, 0)
    for t in range(first + trips * unroll, last):
        step(t)


def read_codes(codes, held):
    row = codes[0:1, :]
    for t in range(held.shape[0]):
        held[t] = row[0, t]


def position(held, t):
    code = held[t]
    return code & 255, (code >> 8) & 255


def given(held, t):
    code = held[t]
    return (code >> 16) & 255, code >> 24


def fold_rows(a):
    return jnp.max(a.reshape(B // 8, 8, B), axis=0)


def lane_peaks(acc, blocks, first, packed):
    lane = lax.broadcasted_iota(jnp.int32, (B, B), 1)
    for b in range(blocks):
        peak = jnp.max(acc[b].astype(F32), axis=1, keepdims=True)
        packed = jnp.where(lane == first + b, peak, packed)
    return packed


def spread_rows(rep, scales):
    n = scales.shape[0]
    turned = jnp.concatenate([scales, jnp.zeros((B - n, B), F32)], axis=0).T
    for b in range(n):
        rep[b] = jnp.broadcast_to(turned[:, b : b + 1], (B, B))


def col_peaks(acc, col_blocks):
    return jnp.concatenate(
        [jnp.max(acc[c], axis=0, keepdims=True) for c in range(col_blocks)], axis=0
    )


def first_peaks(rb, cb, slots, chunk, *refs):
    count, row_hbm, col_hbm, tiles_hbm, dual_hbm = refs[:5]
    payload, scale_col, codes = refs[5:8]
    row, col, held, tiles, racc16, cacc16, racc, sems, index_sems, dual_sem = refs[8:]
    index_copies = [
        pltpu.make_async_copy(row_hbm, row, index_sems.at[0]),
        pltpu.make_async_copy(col_hbm, col, index_sems.at[1]),
    ]
    copies = [
        pltpu.make_async_copy(
            tiles_hbm.at[pl.ds(i * chunk, chunk)], tiles.at[pl.ds(i * chunk, chunk)], sems.at[i]
        )
        for i in range(slots // chunk)
    ]
    dual_copy = pltpu.make_async_copy(dual_hbm, payload.at[pl.ds(2 * rb, dual_hbm.shape[0])], dual_sem)
    for c in index_copies + copies + [dual_copy]:
        c.start()
    racc16[...] = jnp.zeros_like(racc16)
    cacc16[...] = jnp.zeros_like(cacc16)
    racc[...] = jnp.zeros_like(racc)
    for c in index_copies:
        c.wait()
    lane = lax.broadcasted_iota(jnp.int32, codes.shape, 1)
    packed = jnp.zeros(codes.shape, jnp.int32)
    for t in range(slots):
        r, c = row[t], col[t]
        code = jnp.where(t < count[0], r + (c << 8), rb + (cb << 8)) + (r << 16) + (c << 24)
        held[t] = code
        packed = jnp.where(lane == t, code, packed)
    codes[...] = packed

    def plain(t):
        a = jnp.abs(tiles[t])
        r, c = position(held, t)
        racc16[r] = jnp.maximum(racc16[r], a)
        cacc16[c] = jnp.maximum(cacc16[c], jnp.max(a.reshape(B // 16, 16, B), axis=0))

    for i, c in enumerate(copies):
        c.wait()
        loop(i * chunk, (i + 1) * chunk, chunk, plain)
    col_peak = jnp.concatenate(
        [jnp.max(cacc16[c].astype(F32), axis=0, keepdims=True) for c in range(cb)], axis=0
    )
    scale_col[0:cb] = 1.0 / jnp.sqrt(col_peak + EPS)
    scale_col[cb : cb + 1] = jnp.zeros((1, B), F32)

    def scaled(t):
        a = jnp.abs(tiles[t].astype(F32))
        r, c = position(held, t)
        racc[r] = jnp.maximum(racc[r], a * scale_col[pl.ds(c, 1), :])

    loop(0, slots, UNROLL, scaled)
    packed = lane_peaks(racc16, rb, 0, jnp.zeros((B, B), F32))
    packed = lane_peaks(racc, rb, rb, packed)
    payload[0 : 2 * rb] = packed.T[0 : 2 * rb]
    dual_copy.wait()


def second_peaks(rb, cb, slots, pays, *refs):
    codes, tiles, scale_col1, parts = refs[0], refs[1], refs[2], refs[3 : 3 + pays]
    peaks, scale_row2, scale_col3, dual = refs[3 + pays : 7 + pays]
    held, rep, cacc, dacc, scol2, scol3, racc, racc_b = refs[7 + pays :]
    read_codes(codes, held)
    me = lax.axis_index("flt")
    chip, core = me // 2, lax.rem(me, 2)
    peak = parts[0][0 : 2 * rb]
    for p in parts[1:]:
        peak = jnp.maximum(peak, p[0 : 2 * rb])
    srow1 = 1.0 / jnp.sqrt(peak[0:rb] + EPS)
    srow2 = srow1 / jnp.sqrt(srow1 * peak[rb : 2 * rb] + EPS)
    scale_row2[...] = srow2
    spread_rows(rep, jnp.concatenate([srow1, srow2], axis=0))
    scen = dual.shape[1]
    n = 2 * rb
    if pays == 1:
        for i in range(rb):
            dual[i] = parts[0][n + scen * i : n + scen * (i + 1)]
    else:
        mine, first, second, other = [p[n:] for p in parts]
        got = [mine, jnp.where(core == 0, first, other), second, jnp.where(core == 0, other, first)]
        for k, g in enumerate(got):
            for i in range(2):
                dual[2 * (chip ^ k) + i] = g[scen * i : scen * (i + 1)]
    cacc[...] = jnp.zeros_like(cacc)
    dacc[...] = jnp.zeros_like(dacc)
    racc[...] = jnp.zeros_like(racc)
    racc_b[...] = jnp.zeros_like(racc_b)

    def columns(t):
        a = jnp.abs(tiles[t].astype(F32))
        r, c = given(held, t)[0], position(held, t)[1]
        cacc[c] = jnp.maximum(cacc[c], fold_rows(a * rep[r]))
        dacc[c] = jnp.maximum(dacc[c], fold_rows(a * rep[r + rb]))

    loop(0, slots, 24, columns)
    c1 = scale_col1[0:cb]
    c2 = c1 / jnp.sqrt(c1 * col_peaks(cacc, cb) + EPS)
    c3 = c2 / jnp.sqrt(c2 * col_peaks(dacc, cb) + EPS)
    scol2[0:cb] = c2
    scol3[0:cb] = c3
    scol2[cb : cb + 1] = jnp.zeros((1, B), F32)
    scol3[cb : cb + 1] = jnp.zeros((1, B), F32)
    scale_col3[...] = c3

    def rows(t):
        a = jnp.abs(tiles[t].astype(F32))
        r, c = position(held, t)
        racc[r] = jnp.maximum(racc[r], a * scol2[pl.ds(c, 1), :])
        racc_b[r] = jnp.maximum(racc_b[r], a * scol3[pl.ds(c, 1), :])

    loop(0, slots, 24, rows)
    packed = lane_peaks(racc, rb, 0, jnp.zeros((B, B), F32))
    packed = lane_peaks(racc_b, rb, rb, packed)
    peaks[...] = packed.T[0 : 2 * rb]


def pull(slots, held, mat, lhs, gacc):
    gacc[...] = jnp.zeros_like(gacc)

    def step(t):
        r, c = given(held, t)
        gacc[c] += jnp.dot(lhs[r], mat[t], preferred_element_type=F32)

    loop(0, slots, slots, step)


def holds(cb, gacc, offsets, scol, read_hold, write):
    for c in range(cb):
        scale = scol[c : c + 1]
        hold_cost = (HOLD_BASE + COST_RATE * offsets[c : c + 1].astype(F32)) * scale
        hold = read_hold(c, scale)
        hold_next = jnp.clip(hold - TAU_HOLD * (hold_cost + gacc[c]), 0.0, HOLD_CAP / scale)
        write(c, scale, hold_next, 2.0 * hold_next - hold)


def build_step(rb, cb, slots, *refs):
    codes, tiles, srow3, srow4, scale_col3, low, offsets, hold0 = refs[:8]
    mat, scale_col4, hold1, turn, held, rep, cacc, scol, gacc = refs[8:]
    read_codes(codes, held)
    spread_rows(rep, jnp.concatenate([srow3[...], srow4[...]], axis=0))
    cacc[...] = jnp.zeros_like(cacc)

    def columns(t):
        a = jnp.abs(tiles[t].astype(F32))
        r, c = given(held, t)[0], position(held, t)[1]
        cacc[c] = jnp.maximum(cacc[c], fold_rows(a * rep[r]))

    loop(0, slots, UNROLL, columns)
    c3 = scale_col3[...]
    c4 = c3 / jnp.sqrt(c3 * col_peaks(cacc, cb) + EPS)
    scale_col4[...] = c4
    scol[0:cb] = c4

    def build(t):
        r, c = given(held, t)
        live = (position(held, t)[0] < rb).astype(F32)
        value = tiles[t].astype(F32) * live * rep[r + rb] * scol[pl.ds(c, 1), :]
        mat[t] = value.astype(BF16)

    loop(0, slots, UNROLL, build)
    pull(slots, held, mat, low, gacc)

    def write(c, scale, hold, double):
        hold1[:, c * B : (c + 1) * B] = hold
        turn[:, c * B : (c + 1) * B] = double

    holds(
        cb, gacc, offsets, scol, lambda c, scale: hold0[:, c * B : (c + 1) * B] / scale, write
    )


def hold_step(rb, cb, slots, *refs):
    codes, mat, scol, offsets, hold1, low, hold2, turn, held, gacc = refs
    read_codes(codes, held)
    pull(slots, held, mat, low, gacc)

    def write(c, scale, hold, double):
        hold2[:, c * B : (c + 1) * B] = hold * scale
        turn[:, c * B : (c + 1) * B] = double

    holds(cb, gacc, offsets, scol, lambda c, scale: hold1[:, c * B : (c + 1) * B], write)


def plan_step(rb, cb, slots, scen_all, means, split, last, *refs):
    codes, mat, srow4, scol, offsets, capacity, plan, turn, own_dual = refs[:9]
    sums, refs = refs[9 : 9 + means], refs[9 + means :]
    plan_next, loads = refs[0], refs[1 : 1 + split]
    held, lhs, gacc, lacc, mixed = refs[1 + split :]
    read_codes(codes, held)
    me = lax.axis_index("flt")
    chip, core = me // 2, lax.rem(me, 2)
    total = sums[0][...]
    if means > 1:
        first, second, other = [s[...] for s in sums[1:]]
        total = (total + jnp.where(core == 0, first, other)) + (second + jnp.where(core == 0, other, first))
    for b in range(rb):
        lhs[b] = three_terms(total[b : b + 1])
    pull(slots, held, mat, lhs, gacc)
    for c in range(cb):
        scale = scol[c : c + 1]
        cost = COST_RATE * offsets[c : c + 1].astype(F32) * scale
        mean_grad = (gacc[c, 0:1] + gacc[c, 1:2] + gacc[c, 2:3]) / scen_all
        x = plan[c : c + 1] if last else plan[c : c + 1] / scale
        x_next = jnp.clip(x - TAU_PLAN * (cost + mean_grad), 0.0, 1.0 / scale)
        mixed[c] = ((2.0 * x_next - x) + turn[:, c * B : (c + 1) * B]).astype(BF16)
        plan_next[c : c + 1] = x_next
    lacc[...] = jnp.zeros_like(lacc)

    def push(t):
        r, c = given(held, t)
        lacc[r] += lax.dot_general(
            mixed[c], mat[t], (((1,), (1,)), ((), ())), preferred_element_type=F32
        )

    loop(0, slots, slots, push)
    own = srow4[pl.ds(me, 1), :]
    lacc[me] += own_dual[...] * (1.0 / SIGMA) - CAP_UNIT * capacity[...].astype(F32) * own
    if split == 2:
        for k, mine in enumerate((core, 1 - core)):
            via = chip ^ (1 + 2 * mine)
            if last:
                picks = (2 * chip + mine, 2 * via, 2 * via + 1, 2 * (chip ^ 2) + mine)
            else:
                picks = [2 * j + mine for j in range(rb // 2)]
            for j, b in enumerate(picks):
                loads[k][j] = lacc[b]
    else:
        loads[0][...] = lacc[...]


def three_terms(value):
    hi = value.astype(BF16).astype(F32)
    mid = (value - hi).astype(BF16).astype(F32)
    lo = value - hi - mid
    at = lax.broadcasted_iota(jnp.int32, (16, B), 0)
    terms = jnp.where(at == 0, hi, jnp.where(at == 1, mid, jnp.where(at == 2, lo, 0.0)))
    return terms.astype(BF16)


def cross(x, even, odd):
    pairs = [(i, i ^ (odd if i % 2 else even)) for i in range(lax.axis_size("flt"))]
    return lax.ppermute(x, "flt", pairs)


def cross_scn(x, even, odd):
    nf, ns = lax.axis_size("flt"), lax.axis_size("scn")
    pairs = [(f * ns + s, f * ns + (s ^ (odd if f % 2 else even))) for f in range(nf) for s in range(ns)]
    return lax.ppermute(x, ("flt", "scn"), pairs)


def twin(x):
    return lax.ppermute(x, "flt", [(i, i ^ 1) for i in range(lax.axis_size("flt"))])


def interleave(mine, other, core):
    even, odd = jnp.where(core == 0, mine, other), jnp.where(core == 0, other, mine)
    return jnp.stack([even, odd], axis=1).reshape((-1,) + mine.shape[1:])


def in_hbm(x):
    return pltpu.with_memory_space_constraint(x, pltpu.HBM)


def round_low(y):
    rounded = lax.reduce_precision(y, 8, 7)
    return rounded.astype(BF16), jnp.sum(rounded, axis=1)


def body(tiles, tile_row, tile_col, tile_count, slot_offset, capacity, plan0, hold0, dual0):
    slots = tiles.shape[0]
    cb = plan0.shape[0] // B
    nf, ns = lax.axis_size("flt"), lax.axis_size("scn")
    scen = dual0.shape[0]
    rb = nf
    scen_all = scen * ns
    small = nf == 8 and ns == 4
    me = lax.axis_index("flt")
    chip, core = me // 2, me % 2
    offsets = slot_offset.reshape(cb, B)
    f32 = functools.partial(jax.ShapeDtypeStruct, dtype=F32)
    held = [pltpu.SMEM((slots,), jnp.int32)]
    chunk = 12 if slots % 12 == 0 else slots

    mine, scol1, codes = call(
        functools.partial(first_peaks, rb, cb, slots, chunk),
        [f32((2 * rb + scen, B)), f32((cb + 1, B)), jax.ShapeDtypeStruct((8, B), jnp.int32)],
        held * 3
        + [
            pltpu.VMEM((slots, B, B), BF16),
            pltpu.VMEM((rb + 1, B, B), BF16),
            pltpu.VMEM((cb + 1, 16, B), BF16),
            pltpu.VMEM((rb + 1, B, B), F32),
            pltpu.SemaphoreType.DMA((slots // chunk,)),
            pltpu.SemaphoreType.DMA((2,)),
            pltpu.SemaphoreType.DMA,
        ],
        [pl.BlockSpec(memory_space=pltpu.SMEM)] + [HBM] * 4,
    )(tile_count, in_hbm(tile_row), in_hbm(tile_col), in_hbm(tiles), in_hbm(dual0))
    n = 2 * rb
    if small:
        other = twin(mine)
        even = jnp.where(core == 0, mine[n:], other[n:])
        odd = jnp.where(core == 0, other[n:], mine[n:])
        mine = jnp.concatenate([jnp.maximum(mine[:n], other[:n]), even, odd], axis=0)
        first, second = cross(mine, *FIRST), cross(mine, *SECOND)
        best = jnp.maximum(mine[:n], first[:n])
        parts = [mine, first, second, twin(jnp.concatenate([best, first[n:]], axis=0))]
    else:
        gathered = lax.all_gather(mine[n:], "flt", axis=0, tiled=True)
        parts = [jnp.concatenate([lax.pmax(mine[:n], "flt"), gathered], axis=0)]
    peaks, srow2, scol3, dual = call(
        functools.partial(second_peaks, rb, cb, slots, len(parts)),
        [f32((2 * rb, B)), f32((rb, B)), f32((cb, B)), f32((rb, scen, B))],
        held
        + [
            pltpu.VMEM((2 * rb, B, B), F32),
            pltpu.VMEM((cb + 1, 8, B), F32),
            pltpu.VMEM((cb + 1, 8, B), F32),
            pltpu.VMEM((cb + 1, B), F32),
            pltpu.VMEM((cb + 1, B), F32),
            pltpu.VMEM((rb + 1, B, B), F32),
            pltpu.VMEM((rb + 1, B, B), F32),
        ],
        [VMEM] * (3 + len(parts)),
    )(codes, tiles, scol1, *parts)
    if small:
        mine = jnp.maximum(peaks, twin(peaks))
        best, second = jnp.maximum(mine, cross(mine, *FIRST)), cross(mine, *SECOND)
        peak = jnp.maximum(jnp.maximum(best, second), twin(best))
    else:
        peak = lax.pmax(peaks, "flt")
    srow3 = srow2 / jnp.sqrt(srow2 * peak[:rb] + EPS)
    srow4 = srow3 / jnp.sqrt(srow3 * peak[rb:] + EPS)
    own_row = lax.dynamic_slice_in_dim(srow4, me, 1, 0)
    low, sums = round_low(dual / srow4[:, None, :])
    own_dual = dual0 / own_row
    gacc = pltpu.VMEM((cb, scen, B), F32)
    mat, scol4, hold1, turn = call(
        functools.partial(build_step, rb, cb, slots),
        [
            jax.ShapeDtypeStruct((slots, B, B), BF16),
            f32((cb, B)),
            f32((scen, cb * B)),
            f32((scen, cb * B)),
        ],
        held
        + [
            pltpu.VMEM((2 * rb, B, B), F32),
            pltpu.VMEM((cb + 1, 8, B), F32),
            pltpu.VMEM((cb, B), F32),
            gacc,
        ],
        [VMEM] * 8,
    )(codes, tiles, srow3, srow4, scol3, low, offsets, hold0)
    plan = plan0.reshape(cb, B)
    for step in range(2):
        if step:
            if small:
                half = loads[0] + twin(loads[1])
                far = [cross(half, m, m) for m in (2, 4, 6)]
                y = jnp.maximum(SIGMA * ((half + far[0]) + (far[1] + far[2])), 0.0)
                low = y.astype(BF16)
                low = lax.optimization_barrier(interleave(low, twin(low), core))
                sums = jnp.sum(low.astype(F32), axis=1)
                own_dual = lax.dynamic_index_in_dim(y, chip, 0, False)
            else:
                y = jnp.maximum(SIGMA * lax.psum(loads[0], "flt"), 0.0)
                low, sums = round_low(y)
                own_dual = lax.dynamic_index_in_dim(y, me, 0, False)
            hold, turn = call(
                functools.partial(hold_step, rb, cb, slots),
                [f32((scen, cb * B)), f32((scen, cb * B))],
                held + [gacc],
                [VMEM] * 6,
            )(codes, mat, scol4, offsets, hold1, low)
        if small:
            first, second = cross_scn(sums, *FIRST_SCN), cross_scn(sums, *SECOND_SCN)
            first, second, turn = lax.optimization_barrier((first, second, turn))
            totals = [sums, first, second, twin(first)]
        else:
            totals = [lax.psum(sums, "scn")]
        split = 2 if small else 1
        plan, *loads = call(
            functools.partial(
                plan_step, rb, cb, slots, scen_all, len(totals), split, step == 1
            ),
            [f32((cb, B))] + [f32((rb // split, scen, B))] * split,
            held
            + [
                pltpu.VMEM((rb, 16, B), BF16),
                pltpu.VMEM((cb, 16, B), F32),
                pltpu.VMEM((rb, scen, B), F32),
                pltpu.VMEM((cb, scen, B), BF16),
            ],
            [VMEM] * (9 + len(totals)),
        )(codes, mat, srow4, scol4, offsets, capacity, plan, turn, own_dual, *totals)
    if small:
        chip_sum = loads[0] + twin(loads[1])
        first, second = cross(chip_sum[1:3], *FIRST), cross(chip_sum[3], *SECOND)
        own, other = [lax.dynamic_index_in_dim(first, i, 0, False) for i in (core, 1 - core)]
        total = (chip_sum[0] + own) + (second + twin(other))
    else:
        total = lax.psum_scatter(loads[0], "flt", scatter_dimension=0, tiled=False)
    dual = jnp.maximum(SIGMA * total, 0.0) * own_row
    return (plan * scol4).reshape(-1), hold, dual


def solution(mesh):
    return jax.shard_map(
        body,
        mesh=mesh,
        in_specs=(
            P("flt", None, None),
            P("flt"),
            P("flt"),
            P("flt"),
            P("flt"),
            P("scn", "flt"),
            P("flt"),
            P("scn", "flt"),
            P("scn", "flt"),
        ),
        out_specs=(P("flt"), P("scn", "flt"), P("scn", "flt")),
        check_vma=False,
    )
```
